32 devices in a mesh: dp: 4 (over y, x), seq: 4 (over z), tensor: 2 (over core).
Axes of the slice: x: 2, y: 2, z: 4, core: 2. Of those that a mesh axis runs over, the one named last changes fastest.
Arguments:
- tokens: bfloat16 [4, 2048, 2048], P('dp', ('seq', 'tensor')), may hold values from -6 to 6
- lengths: int32 [4, 6], P('dp'), may hold values from 1 to 2043, as said below
- ln1_gain: float32 [2048], replicated, may hold values from 0.5 to 1.5
- ln1_bias: float32 [2048], replicated, may hold values from -4 to 4
- w_query: bfloat16 [2048, 2048], P(None, 'tensor'), may hold values from -0.1875 to 0.1875
- b_query: float32 [16, 128], P('tensor'), may hold values from -6 to 6
- w_key: bfloat16 [2048, 128], replicated, may hold values from -0.1875 to 0.1875
- w_value: bfloat16 [2048, 128], replicated, may hold values from -0.125 to 0.125
- b_value: float32 [128], replicated, may hold values from -6 to 6
- w_out: bfloat16 [2048, 2048], P('tensor'), may hold values from -1 to 1
- b_out: float32 [2048], replicated, may hold values from -4 to 4
- ln2_gain: float32 [2048], replicated, may hold values from 0.5 to 1.5
- ln2_bias: float32 [2048], replicated, may hold values from -4 to 4
- w_up: bfloat16 [2048, 8192], P(None, 'tensor'), may hold values from -0.125 to 0.125
- b_up: float32 [64, 128], P('tensor'), may hold values from -6 to 6
- w_down: bfloat16 [8192, 2048], P('tensor'), may hold values from -0.0625 to 0.0625
- b_down: float32 [2048], replicated, may hold values from -4 to 4
- cotangent: bfloat16 [4, 2048, 2048], P('dp', ('seq', 'tensor')), may hold values from -6 to 6
Outputs:
- output: bfloat16 [4, 2048, 2048], P('dp', ('seq', 'tensor'))
- grad_input: bfloat16 [4, 2048, 2048], P('dp', ('seq', 'tensor'))
- grad_ln1_gain: float32 [2048], P(('dp', 'seq', 'tensor'))
- grad_ln1_bias: float32 [2048], P(('dp', 'seq', 'tensor'))
- grad_w_query: float32 [2048, 2048], P(('dp', 'seq'), 'tensor')
- grad_b_query: float32 [16, 128], P('tensor', ('dp', 'seq'))
- grad_w_key: float32 [2048, 128], P(('dp', 'seq', 'tensor'))
- grad_w_value: float32 [2048, 128], P(('dp', 'seq', 'tensor'))
- grad_b_value: float32 [128], P(('dp', 'seq', 'tensor'))
- grad_w_out: float32 [2048, 2048], P('tensor', ('dp', 'seq'))
- grad_b_out: float32 [2048], P(('dp', 'seq', 'tensor'))
- grad_ln2_gain: float32 [2048], P(('dp', 'seq', 'tensor'))
- grad_ln2_bias: float32 [2048], P(('dp', 'seq', 'tensor'))
- grad_w_up: float32 [2048, 8192], P(('dp', 'seq'), 'tensor')
- grad_b_up: float32 [64, 128], P('tensor', ('dp', 'seq'))
- grad_w_down: float32 [8192, 2048], P('tensor', ('dp', 'seq'))
- grad_b_down: float32 [2048], P(('dp', 'seq', 'tensor'))
The draws below stay inside these ranges and needn't reach their ends.
Inputs may be any that keep to these rules, and one draw needn't show every extreme that they name: Each window's lengths are positive and sum to 2048; one of them, at a position drawn for each window, is larger than 1536, and each other one is at most (511) // 5. In one window, drawn from the seed, every other length is 1.
All inputs are finite; a program needn't handle non-finite values.
Results may differ from the reference program's by a relative error of at most 0.017.
Values may be sent and summed in bfloat16 or wider, within the bound.
No kernel may reach another device: no remote copies, remote signals or barrier semaphores. Data moves between devices by JAX's collectives and lax.ppermute only.
A program may use at most 256 MiB of HBM per device.

```python
import jax
import jax.numpy as jnp
from jax import lax

D = 2048
HEADS = 16
HEAD = 128
FF = 8192
TOK_DEV = 512
DOCS = 6
QW = 2048
FB = 64
WINDOWS = 4
LEN = 2048


def draw_lengths(key, part):
    key = jax.random.fold_in(key, 11)
    first_key, second_key, third_key = jax.random.split(key, 3)
    others = jax.random.randint(first_key, (WINDOWS, DOCS - 1), 1, (TOK_DEV - 1) // (DOCS - 1) + 1, dtype=jnp.int32)
    single = jax.random.randint(third_key, (), 0, WINDOWS, dtype=jnp.int32)
    window_ids = jnp.arange(WINDOWS, dtype=jnp.int32)[:, None]
    others = jnp.where(window_ids == single, jnp.ones_like(others), others)
    longest = LEN - jnp.sum(others, axis=1)
    where_long = jax.random.randint(second_key, (WINDOWS,), 0, DOCS, dtype=jnp.int32)
    slots = jnp.arange(DOCS, dtype=jnp.int32)[None, :]
    source = jnp.where(slots < where_long[:, None], slots, slots - 1)
    source = jnp.clip(source, 0, DOCS - 2)
    picked = jnp.take_along_axis(others, source, axis=1)
    return jnp.where(slots == where_long[:, None], longest[:, None], picked).astype(jnp.int32)


def steps_of(own_key, dims, cuts, low, top_value):
    def one(position, blocks):
        heights = jax.random.uniform(jax.random.fold_in(jax.random.fold_in(own_key, 6), position), (blocks,), jnp.float32, low / len(cuts), top_value / len(cuts))
        return jnp.repeat(jnp.exp(heights), dims[position] // blocks).reshape((-1,) + (1,) * (len(dims) - position - 1))

    loudness = one(*cuts[0])
    for cut in cuts[1:]:
        loudness = loudness * one(*cut)
    return loudness


def noise(own_key, dims, scale, most, cuts=(), held_as=jnp.bfloat16):
    result = scale * jax.random.normal(own_key, dims, jnp.float32)
    if cuts:
        result = result * steps_of(own_key, dims, cuts, -0.22, 0.18)
    return jnp.clip(result, -most, most).astype(held_as)


def setup_inputs(seed: int = 0) -> dict:
    key_of = jax.random.split(jax.random.key(seed), 19)
    return {
        "tokens": noise(key_of[0], (WINDOWS, LEN, D), 1.0, 6.0, ((0, 4), (1, 8))),
        "lengths": draw_lengths(jax.random.fold_in(key_of[18], 71), 0),
        "ln1_gain": jnp.clip(1.0 + 0.1 * jax.random.normal(key_of[2], (D,), jnp.float32), 0.5, 1.5),
        "ln1_bias": noise(key_of[3], (D,), 0.3, 4.0, (), jnp.float32),
        "w_query": noise(key_of[4], (D, QW), (D // 2) ** -0.5, 0.1875, ((1, 2),)),
        "b_query": noise(key_of[5], (HEADS, HEAD), 0.5, 6.0, ((0, 2),), jnp.float32),
        "w_key": noise(key_of[6], (D, HEAD), (D // 2) ** -0.5, 0.1875),
        "w_value": noise(key_of[7], (D, HEAD), D ** -0.5, 0.125),
        "b_value": noise(key_of[8], (HEAD,), 0.5, 6.0, (), jnp.float32),
        "w_out": noise(key_of[9], (QW, D), (QW // 64) ** -0.5, 1.0, ((0, 2),)),
        "b_out": noise(key_of[10], (D,), 0.3, 4.0, (), jnp.float32),
        "ln2_gain": jnp.clip(1.0 + 0.1 * jax.random.normal(key_of[11], (D,), jnp.float32), 0.5, 1.5),
        "ln2_bias": noise(key_of[12], (D,), 0.3, 4.0, (), jnp.float32),
        "w_up": noise(key_of[13], (D, FF), D ** -0.5, 0.125, ((1, 2),)),
        "b_up": noise(key_of[14], (FB, 128), 0.5, 6.0, ((0, 2),), jnp.float32),
        "w_down": noise(key_of[15], (FF, D), FF ** -0.5, 0.0625, ((0, 2),)),
        "b_down": noise(key_of[16], (D,), 0.3, 4.0, (), jnp.float32),
        "cotangent": noise(key_of[17], (WINDOWS, LEN, D), 1.0, 6.0, ((0, 4), (1, 8))),
    }


epsilon = 1e-05
negative = -1e+30

@jax.custom_vjp
def low(v):
    return lax.optimization_barrier(v.astype(jnp.bfloat16)).astype(jnp.float32)

@jax.custom_vjp
def low_back(v):
    return v

def low_keep(v):
    return (low(v), None)

def low_pass(kept, grad):
    return (grad,)

def back_keep(v):
    return (v, None)

def back_low(kept, grad):
    return (low(grad),)
low.defvjp(low_keep, low_pass)
low_back.defvjp(back_keep, back_low)

def layer_norm(rows, gain, shift):
    centre = rows - lax.optimization_barrier(jnp.mean(rows, axis=-1, keepdims=True))
    spread = lax.optimization_barrier(jnp.mean(centre * centre, axis=-1, keepdims=True))
    return centre * lax.rsqrt(spread + epsilon) * gain + shift

def product(left, right):
    return jnp.dot(left, right, precision=lax.Precision.HIGHEST)

def attend(query, keys, values, segment):
    length = query.shape[0]
    rows = min(512, length)
    count = length // rows
    query_blocks = query.reshape(count, rows, HEADS, HEAD)
    key_pos = jnp.arange(length, dtype=jnp.int32)

    def one_block(inputs):
        block_query, index = inputs
        query_pos = index * rows + jnp.arange(rows, dtype=jnp.int32)
        query_seg = lax.dynamic_slice_in_dim(segment, index * rows, rows)
        allowed = (key_pos[None, :] <= query_pos[:, None]) & (segment[None, :] == query_seg[:, None])
        scores = low_back(jnp.einsum('qhd,kd->qhk', block_query, keys, precision=lax.Precision.HIGHEST) * HEAD ** (-0.5))
        scores = jnp.where(allowed[:, None, :], scores, negative)
        highest = lax.optimization_barrier(jnp.max(scores, axis=2, keepdims=True))
        log_total = highest + jnp.log(lax.optimization_barrier(jnp.sum(jnp.exp(scores - highest), axis=2, keepdims=True)))
        probs = low(jnp.exp(scores - log_total))
        return jnp.einsum('qhk,kd->qhd', probs, values, precision=lax.Precision.HIGHEST)
    blocks = lax.map(jax.checkpoint(one_block), (query_blocks, jnp.arange(count, dtype=jnp.int32)))
    return blocks.reshape(length, HEADS * HEAD)

def window_layer(params, row_input, segment):
    gain_one, shift_one, w_query, b_query, w_key, w_value, b_value, w_out, b_out, gain_two, shift_two, w_up, b_up, w_down, b_down = params
    normed = low(layer_norm(row_input, gain_one, shift_one))
    query = low(low_back(product(normed, w_query) + b_query.reshape(-1)))
    keys = low(low_back(product(normed, w_key)))
    values = low(low_back(product(normed, w_value) + b_value))
    attended = low(low_back(attend(query, keys, values, segment)))
    middle = row_input + low_back(product(attended, w_out) + b_out)
    normed_two = low(layer_norm(middle, gain_two, shift_two))
    hidden = low_back(product(normed_two, w_up) + b_up.reshape(-1))
    activated = low(jax.nn.gelu(hidden, approximate=True))
    return middle + low_back(product(activated, w_down) + b_down)

def reference(tokens, lengths, ln1_gain, ln1_bias, w_query, b_query, w_key, w_value, b_value, w_out, b_out, ln2_gain, ln2_bias, w_up, b_up, w_down, b_down, cotangent):
    ends = jnp.cumsum(lengths, axis=1, dtype=jnp.int32)
    positions = jnp.arange(LEN, dtype=jnp.int32)
    segment = lax.optimization_barrier(jnp.sum((positions[None, :, None] >= ends[:, None, :]).astype(jnp.int32), axis=2)).astype(jnp.int32)
    params = tuple((item.astype(jnp.float32) for item in (ln1_gain, ln1_bias, w_query, b_query, w_key, w_value, b_value, w_out, b_out, ln2_gain, ln2_bias, w_up, b_up, w_down, b_down)))

    def forward(inputs, weights):
        return lax.map(lambda couple: window_layer(weights, couple[0], couple[1]), (inputs, segment))
    output, pull = jax.vjp(forward, tokens.astype(jnp.float32), params)
    grad_inputs, grads = pull(cotangent.astype(jnp.float32))
    return (output.astype(jnp.bfloat16), grad_inputs.astype(jnp.bfloat16), grads[0], grads[1], grads[2], grads[3], grads[4], grads[5], grads[6], grads[7], grads[8], grads[9], grads[10], grads[11], grads[12], grads[13], grads[14])
```

```python
import functools

import jax
import jax.numpy as jnp
from jax import lax
from jax.experimental import pallas as pl
from jax.experimental.pallas import tpu as pltpu
from jax.sharding import PartitionSpec as P

epsilon = 1e-05
negative = -1e30
log2e = 1.4426950408889634
f32 = jnp.float32
low = jnp.bfloat16
vmem_bytes = 48 * 1024 * 1024


def dot(left, right):
    return jnp.dot(left, right, preferred_element_type=f32)


def contract_rows(left, right):
    return lax.dot_general(left, right, (((0,), (0,)), ((), ())), preferred_element_type=f32)


def contract_cols(left, right):
    return lax.dot_general(left, right, (((1,), (1,)), ((), ())), preferred_element_type=f32)


def allowed_mask(start, base, flip, pos_ref):
    offset = lax.broadcasted_iota(jnp.int32, (start, 1), 0)
    key_pos = base + (offset ^ flip)
    return (key_pos <= pos_ref[0:1, :]) & (key_pos >= pos_ref[1:2, :])


def over_blocks(info, body):
    body(0, True)
    lax.fori_loop(1, info[0], lambda s, c: (body(s, False), c)[1], 0)
    lax.fori_loop(info[0], info[1], lambda s, c: (body(s, True), c)[1], 0)


def attend_kernel(
    scale, info, q_ref, k_ref, vt_ref, pos_ref, o_ref, lse_ref, m_ref, l_ref, acc_ref
):
    span = q_ref.shape[0]
    head = k_ref.shape[1]
    pair = q_ref.shape[1] // head
    step = pl.program_id(0)
    turned = [q_ref[:, h * head : (h + 1) * head].T for h in range(pair)]
    m_ref[...] = jnp.full_like(m_ref, negative)
    l_ref[...] = jnp.zeros_like(l_ref)
    acc_ref[...] = jnp.zeros_like(acc_ref)

    def body(s, masked):
        where = pl.multiple_of(s * span, span)
        key_block = k_ref[pl.ds(where, span), :]
        value_block = vt_ref[:, pl.ds(where, span)]
        if masked:
            allowed = allowed_mask(span, (info[2] - s) * span, info[3], pos_ref)
        for h in range(pair):
            scores = dot(key_block, turned[h]) * scale
            if masked:
                scores = jnp.where(allowed, scores, negative)
            before = m_ref[h]
            after = jnp.maximum(before, jnp.max(scores, axis=0, keepdims=True))
            weights = jnp.exp2(scores - after)
            shrink = jnp.exp2(before - after)
            m_ref[h] = after
            l_ref[h] = l_ref[h] * shrink + jnp.sum(weights, axis=0, keepdims=True)
            acc_ref[h] = acc_ref[h] * shrink + dot(value_block, weights.astype(low))

    over_blocks(info, body)
    for h in range(pair):
        total = l_ref[h]
        lse_ref[pl.ds(step * pair + h, 1), :] = m_ref[h] + jnp.log2(total)
        o_ref[:, h * head : (h + 1) * head] = (acc_ref[h] / total).T.astype(low)


def attend_back_kernel(
    scale,
    unit,
    info,
    q_ref,
    do_ref,
    o_ref,
    lse_ref,
    k_ref,
    kt_ref,
    v_ref,
    pos_ref,
    dq_ref,
    dkv_ref,
    dk_ref,
    dv_ref,
    dqt_ref,
):
    span = q_ref.shape[0]
    head = k_ref.shape[1]
    pair = q_ref.shape[1] // head
    step = pl.program_id(0)

    @pl.when(step == 0)
    def _():
        dk_ref[...] = jnp.zeros_like(dk_ref)
        dv_ref[...] = jnp.zeros_like(dv_ref)

    dqt_ref[...] = jnp.zeros_like(dqt_ref)
    queries = [q_ref[:, h * head : (h + 1) * head] for h in range(pair)]
    grads = [do_ref[:, h * head : (h + 1) * head] for h in range(pair)]
    queries_t = [item.T for item in queries]
    grads_t = [item.T for item in grads]
    inner = [
        jnp.sum(
            grads_t[h].astype(f32) * o_ref[:, h * head : (h + 1) * head].T.astype(f32),
            axis=0,
            keepdims=True,
        )
        for h in range(pair)
    ]
    totals = [lse_ref[pl.ds(step * pair + h, 1), :] for h in range(pair)]

    def body(s, masked):
        where = pl.multiple_of(s * span, span)
        key_block = k_ref[pl.ds(where, span), :]
        key_turned = kt_ref[:, pl.ds(where, span)]
        value_block = v_ref[pl.ds(where, span), :]
        if masked:
            allowed = allowed_mask(span, (info[2] - s) * span, info[3], pos_ref)
        key_part = jnp.zeros((span, head), f32)
        value_part = jnp.zeros((span, head), f32)
        for h in range(pair):
            scores = dot(key_block, queries_t[h]) * scale - totals[h]
            if masked:
                scores = jnp.where(allowed, scores, negative)
            probs = jnp.exp2(scores)
            grad_probs = dot(value_block, grads_t[h])
            grad_scores = (probs * (grad_probs - inner[h])).astype(low)
            key_part += dot(grad_scores, queries[h])
            value_part += dot(probs.astype(low), grads[h])
            dqt_ref[h] += dot(key_turned, grad_scores)
        dk_ref[pl.ds(where, span), :] += key_part
        dv_ref[pl.ds(where, span), :] += value_part

    over_blocks(info, body)
    for h in range(pair):
        dq_ref[:, h * head : (h + 1) * head] = (dqt_ref[h] * unit).T.astype(low)

    @pl.when(step == pl.num_programs(0) - 1)
    def _():
        dkv_ref[0] = (dk_ref[...] * unit).astype(low)
        dkv_ref[1] = dv_ref[...].astype(low)


def attend(info, query, keys, values_t, pos, heads, head):
    span = query.shape[0]
    window = keys.shape[0]
    pair = 2
    scale = head**-0.5 * log2e
    work = heads * span * window * head
    spec = pltpu.PrefetchScalarGridSpec(
        num_scalar_prefetch=1,
        grid=(heads // pair,),
        in_specs=[
            pl.BlockSpec((span, pair * head), lambda i, s: (0, i)),
            pl.BlockSpec((window, head), lambda i, s: (0, 0)),
            pl.BlockSpec((head, window), lambda i, s: (0, 0)),
            pl.BlockSpec(pos.shape, lambda i, s: (0, 0)),
        ],
        out_specs=[
            pl.BlockSpec((span, pair * head), lambda i, s: (0, i)),
            pl.BlockSpec((heads, span), lambda i, s: (0, 0)),
        ],
        scratch_shapes=[
            pltpu.VMEM((pair, 1, span), f32),
            pltpu.VMEM((pair, 1, span), f32),
            pltpu.VMEM((pair, head, span), f32),
        ],
    )
    return pl.pallas_call(
        functools.partial(attend_kernel, scale),
        grid_spec=spec,
        out_shape=(
            jax.ShapeDtypeStruct(query.shape, low),
            jax.ShapeDtypeStruct((heads, span), f32),
        ),
        compiler_params=pltpu.CompilerParams(vmem_limit_bytes=vmem_bytes),
        cost_estimate=pl.CostEstimate(
            flops=8 * work, bytes_accessed=4 * query.size, transcendentals=work // head
        ),
        name="attend",
    )(info, query, keys, values_t, pos)


def attend_back(info, query, grad, attended, lse, keys, keys_t, values, pos, heads, head):
    span = query.shape[0]
    window = keys.shape[0]
    pair = 2
    scale = head**-0.5 * log2e
    work = heads * span * window * head
    wide = pl.BlockSpec((span, pair * head), lambda i, s: (0, i))
    tall = pl.BlockSpec((window, head), lambda i, s: (0, 0))
    spec = pltpu.PrefetchScalarGridSpec(
        num_scalar_prefetch=1,
        grid=(heads // pair,),
        in_specs=[
            wide,
            wide,
            wide,
            pl.BlockSpec((heads, span), lambda i, s: (0, 0)),
            tall,
            pl.BlockSpec((head, window), lambda i, s: (0, 0)),
            tall,
            pl.BlockSpec(pos.shape, lambda i, s: (0, 0)),
        ],
        out_specs=[wide, pl.BlockSpec((2, window, head), lambda i, s: (0, 0, 0))],
        scratch_shapes=[
            pltpu.VMEM((window, head), f32),
            pltpu.VMEM((window, head), f32),
            pltpu.VMEM((pair, head, span), f32),
        ],
    )
    return pl.pallas_call(
        functools.partial(attend_back_kernel, scale, head**-0.5),
        grid_spec=spec,
        out_shape=(
            jax.ShapeDtypeStruct(query.shape, low),
            jax.ShapeDtypeStruct((2, window, head), low),
        ),
        compiler_params=pltpu.CompilerParams(vmem_limit_bytes=vmem_bytes),
        cost_estimate=pl.CostEstimate(
            flops=20 * work, bytes_accessed=8 * query.size, transcendentals=work // head
        ),
        name="attend_back",
    )(info, query, grad, attended, lse, keys, keys_t, values, pos)


def swap(item):
    return lax.ppermute(item, "tensor", [(0, 1), (1, 0)])


def cross(item, bits):
    size = lax.axis_size("dp")
    return lax.ppermute(item, "dp", [(i, i ^ bits) for i in range(size)])


def shift(item, by):
    size = lax.axis_size("seq")
    return lax.ppermute(item, "seq", [(i, (i + by) % size) for i in range(size)])


def shift_up(item, by):
    size = lax.axis_size("seq")
    return lax.ppermute(item, "seq", [(i, i + by) for i in range(size - by)])


def shift_down(item, by):
    size = lax.axis_size("seq")
    return lax.ppermute(item, "seq", [(i + by, i) for i in range(size - by)])


def pair_gather(item):
    return jnp.concatenate([item, swap(item)], axis=0)


def pair_sum(left, right_of):
    half = left.shape[0] // 2
    mine = right_of(left[:half])
    theirs = right_of(left[half:]).astype(low)
    return mine + swap(theirs).astype(f32)


def ring_gather(own):
    size = lax.axis_size("seq")
    held, blocks = own, []
    for step in range(size):
        if step:
            held = shift(held, 1)
        blocks.append(pair_gather(held))
    return blocks


def dp_scatter(piece):
    far = piece(3).astype(low)
    half = far.shape[0] // 2
    near_x = piece(1).astype(low)
    near_y = piece(2).astype(low)
    far_a = cross(far[:half], 1)
    far_b = cross(far[half:], 2)
    own_a = cross(near_x[:half], 1)
    own_b = cross(near_y[half:], 2)
    own = piece(0)
    second_a = (near_y[:half].astype(f32) + far_a.astype(f32)).astype(low)
    second_b = (near_x[half:].astype(f32) + far_b.astype(f32)).astype(low)
    got_a = cross(second_a, 2)
    got_b = cross(second_b, 1)
    return jnp.concatenate(
        [
            own[:half] + own_a.astype(f32) + got_a.astype(f32),
            own[half:] + own_b.astype(f32) + got_b.astype(f32),
        ],
        axis=0,
    )


def norm_parts(rows):
    centre = rows - jnp.mean(rows, axis=-1, keepdims=True)
    inverse = lax.rsqrt(jnp.mean(centre * centre, axis=-1, keepdims=True) + epsilon)
    return centre * inverse, inverse


def norm_back(grad, unit, inverse, gain):
    scaled = grad * gain
    part = (
        scaled
        - jnp.mean(scaled, axis=-1, keepdims=True)
        - unit * jnp.mean(scaled * unit, axis=-1, keepdims=True)
    )
    return part * inverse, jnp.sum(grad * unit, axis=0), jnp.sum(grad, axis=0)


def gelu_both(value, grad):
    inside = 0.7978845608028654 * (value + 0.044715 * value * value * value)
    bend = jnp.tanh(inside)
    half = 0.5 * (1.0 + bend)
    slope = half + 0.5 * value * (1.0 - bend * bend) * 0.7978845608028654 * (
        1.0 + 3.0 * 0.044715 * value * value
    )
    return (value * half).astype(low), (grad.astype(f32) * slope).astype(low)


def on_device(
    tokens,
    lengths,
    ln1_gain,
    ln1_bias,
    w_query,
    b_query,
    w_key,
    w_value,
    b_value,
    w_out,
    b_out,
    ln2_gain,
    ln2_bias,
    w_up,
    b_up,
    w_down,
    b_down,
    cotangent,
):
    shard = tokens[0].astype(f32)
    rows_own, width = shard.shape
    seqs = lax.axis_size("seq")
    dps = lax.axis_size("dp")
    span = 2 * rows_own
    heads, head = b_query.shape
    at_dp, at_seq, at_core = (lax.axis_index(name) for name in ("dp", "seq", "tensor"))
    flip = at_core * rows_own
    span_start = at_seq * span
    hidden_local = w_up.shape[1]
    hidden_part = hidden_local // seqs
    dp_part = width // dps
    out_part = dp_part // seqs

    ends = jnp.cumsum(lengths[0], dtype=jnp.int32)
    row_pos = span_start + (jnp.arange(span, dtype=jnp.int32) ^ flip)
    row_start = jnp.max(
        jnp.where(row_pos[:, None] >= ends[None, :], ends[None, :], 0), axis=1
    ).astype(jnp.int32)
    pos = jnp.zeros((8, span), jnp.int32).at[0].set(row_pos).at[1].set(row_start)
    first, last = jnp.min(row_start), jnp.max(row_start)
    whole_to = jnp.clip(at_seq + 1 - (last + span - 1) // span, 1, at_seq + 1)
    some_to = jnp.clip(at_seq + 1 - first // span, whole_to, at_seq + 1)
    info = jnp.stack([whole_to, some_to, at_seq, flip]).astype(jnp.int32)

    grad_own = cotangent[0]
    grad_blocks = ring_gather(grad_own)
    up_part = lax.dynamic_slice_in_dim(w_up, at_seq * hidden_part, hidden_part, 1)
    down_part = lax.dynamic_slice_in_dim(w_down, at_seq * hidden_part, hidden_part, 0)
    bias_part = lax.dynamic_slice_in_dim(
        b_up.reshape(-1), at_seq * hidden_part, hidden_part, 0
    )
    grad_act = contract_cols(grad_blocks[0], w_down).astype(low)
    grad_act_parts = [
        contract_cols(block, down_part).astype(low) for block in grad_blocks[1:]
    ]

    unit_one, inverse_one = norm_parts(shard)
    normed = (unit_one * ln1_gain + ln1_bias).astype(low)
    key_own = dot(normed, w_key).astype(low)
    value_own = (dot(normed, w_value) + b_value).astype(low)
    both_own = jnp.concatenate([key_own, value_own], axis=1)
    both = [both_own] + [shift_up(both_own, by) for by in range(1, seqs)]
    both = jnp.stack(both)
    both = jnp.stack([both, swap(both)], axis=1).reshape(seqs * span, 2 * head)
    keys, values = both[:, :head], both[:, head:]
    normed_all = pair_gather(normed)
    query = (dot(normed_all, w_query) + b_query.reshape(-1)).astype(low)
    attended, lse = attend(info, query, keys, values.T, pos, heads, head)
    middle = shard + (pair_sum(attended, lambda part: dot(part, w_out)) + b_out)
    unit_two, inverse_two = norm_parts(middle)
    normed_two = (unit_two * ln2_gain + ln2_bias).astype(low)

    normed_blocks = ring_gather(normed_two)
    hidden = dot(normed_blocks[0], w_up) + b_up.reshape(-1)
    activated, grad_hidden = gelu_both(hidden, grad_act)
    result = middle + (pair_sum(activated, lambda part: dot(part, w_down)) + b_down)
    output = result.astype(low)[None]
    grad_normed_two = pair_sum(grad_hidden, lambda part: contract_cols(part, w_up))
    grad_b_up = jnp.sum(grad_hidden.astype(f32), axis=0)

    back, grad_ln2_gain, grad_ln2_bias = norm_back(
        grad_normed_two, unit_two, inverse_two, ln2_gain
    )
    grad_out = grad_own.astype(f32)
    grad_b_down = jnp.sum(grad_out, axis=0)
    grad_middle = grad_out + back
    grad_branch = grad_middle.astype(low)
    grad_b_out = jnp.sum(grad_branch.astype(f32), axis=0)
    grad_branch_all = pair_gather(grad_branch)
    grad_attended = contract_cols(grad_branch_all, w_out).astype(low)

    grad_query, grad_both = attend_back(
        info, query, grad_attended, attended, lse, keys, keys.T, values, pos, heads, head
    )
    grad_both = grad_both.reshape(2, seqs, 2, rows_own, head)
    kept = lax.dynamic_index_in_dim(grad_both, at_core, 0, False)
    given = lax.dynamic_index_in_dim(grad_both, 1 - at_core, 0, False)
    grad_kv = (kept.astype(f32) + swap(given)[:, ::-1].astype(f32)).astype(low)
    grad_kv = grad_kv.reshape(seqs, span, head)
    total = grad_kv[0].astype(f32)
    for by in range(1, seqs):
        total = total + shift_down(grad_kv[by], by).astype(f32)
    grad_kv = total.astype(low)
    grad_qkv = jnp.concatenate([grad_query, grad_kv], axis=1)
    w_qkv = jnp.concatenate([w_query, jnp.where(at_core == 0, w_key, w_value)], axis=1)
    grad_normed = pair_sum(grad_qkv, lambda part: contract_cols(part, w_qkv))
    back, grad_ln1_gain, grad_ln1_bias = norm_back(
        grad_normed, unit_one, inverse_one, ln1_gain
    )
    grad_input = (grad_middle + back).astype(low)[None]

    acts, grads = [], []
    for step in range(seqs):
        if step:
            value = dot(normed_blocks[step], up_part) + bias_part
            act, grad = gelu_both(value, grad_act_parts[step - 1])
        else:
            act = lax.dynamic_slice_in_dim(activated, at_seq * hidden_part, hidden_part, 1)
            grad = lax.dynamic_slice_in_dim(grad_hidden, at_seq * hidden_part, hidden_part, 1)
        acts.append(act)
        grads.append(grad)
    acts = jnp.concatenate(acts, axis=0)
    grads = jnp.concatenate(grads, axis=0)
    grad_tokens = jnp.concatenate(grad_blocks, axis=0)
    normed_tokens = jnp.concatenate(normed_blocks, axis=0)

    def columns(item, r):
        return lax.dynamic_slice_in_dim(item, (at_dp ^ r) * dp_part, dp_part, 1)

    sum_down = dp_scatter(lambda r: contract_rows(acts, columns(grad_tokens, r)))
    sum_up = dp_scatter(lambda r: contract_rows(columns(normed_tokens, r), grads))
    sum_out = dp_scatter(lambda r: contract_rows(attended, columns(grad_branch_all, r)))
    sum_qkv = dp_scatter(lambda r: contract_rows(columns(normed_all, r), grad_qkv))

    def to_seq(item, by, axis):
        at = lax.rem(at_seq + by, seqs)
        return lax.dynamic_slice_in_dim(item, at * out_part, out_part, axis)

    def spread(item, axis):
        narrow = item.astype(low)
        other = 1 - axis
        shape = [out_part, out_part]
        shape[other] = hidden_local
        whole = jnp.zeros(shape, f32)
        for by in range(seqs):
            if by:
                got = shift(to_seq(narrow, by, axis), by).astype(f32)
            else:
                got = to_seq(item, 0, axis)
            at = lax.rem(at_seq + seqs - by, seqs)
            whole = lax.dynamic_update_slice_in_dim(whole, got, at * hidden_part, other)
        return whole

    def seq_sum(item, axis):
        narrow = item.astype(low)
        total = to_seq(item, 0, axis)
        for by in range(1, seqs):
            total = total + shift(to_seq(narrow, by, axis), by).astype(f32)
        return total

    out_w_down = spread(sum_down, 1)
    out_w_up = spread(sum_up, 0)
    out_w_out = seq_sum(sum_out, 1)
    out_qkv = seq_sum(sum_qkv, 0)
    out_w_query = out_qkv[:, : heads * head]
    half = out_part // 2
    last_kv = out_qkv[:, heads * head :]
    mine = lax.dynamic_slice_in_dim(last_kv, at_core * half, half, 0)
    other = swap(lax.dynamic_slice_in_dim(last_kv, (1 - at_core) * half, half, 0))
    out_w_key = jnp.where(at_core == 0, mine, other)
    out_w_value = jnp.where(at_core == 0, other, mine)

    grad_b_value = jnp.where(at_core == 1, jnp.sum(grad_kv.astype(f32), axis=0), 0.0)
    grad_b_query = jnp.sum(grad_query.astype(f32), axis=0)
    shared = [
        item.reshape(dps, seqs, 2, -1)
        for item in (
            grad_ln1_gain,
            grad_ln1_bias,
            grad_b_out,
            grad_ln2_gain,
            grad_ln2_bias,
            grad_b_down,
            grad_b_value,
        )
    ]
    sizes = [item.shape[-1] for item in shared]
    shared = jnp.concatenate(shared, axis=-1)
    shared = lax.dynamic_index_in_dim(shared, at_core, 2, False) + swap(
        lax.dynamic_index_in_dim(shared, 1 - at_core, 2, False)
    )

    def by_device(item, rows):
        item = item.reshape(rows, dps, seqs, -1)
        return jnp.transpose(item, (1, 2, 0, 3)).reshape(dps, seqs, -1)

    local_up = by_device(grad_b_up, b_up.shape[0])
    local_query = by_device(grad_b_query, heads)
    sizes = sizes + [local_up.shape[-1], local_query.shape[-1]]
    packed = jnp.concatenate([shared, local_up, local_query], axis=-1)
    total = lax.dynamic_index_in_dim(packed, at_dp, 0, False)
    for r in (1, 2, 3):
        total = total + cross(lax.dynamic_index_in_dim(packed, at_dp ^ r, 0, False), r)
    packed = total
    total = lax.dynamic_index_in_dim(packed, at_seq, 0, False)
    for by in range(1, seqs):
        at = lax.rem(at_seq + by, seqs)
        total = total + shift(lax.dynamic_index_in_dim(packed, at, 0, False), by)
    parts, at = [], 0
    for size in sizes:
        parts.append(total[at : at + size])
        at += size
    return (
        output,
        grad_input,
        parts[0],
        parts[1],
        out_w_query,
        parts[8].reshape(heads, -1),
        out_w_key,
        out_w_value,
        parts[6],
        out_w_out,
        parts[2],
        parts[3],
        parts[4],
        out_w_up,
        parts[7].reshape(b_up.shape[0], -1),
        out_w_down,
        parts[5],
    )


def solution(mesh):
    in_specs = (
        P("dp", ("seq", "tensor"), None),
        P("dp", None),
        P(),
        P(),
        P(None, "tensor"),
        P("tensor", None),
        P(),
        P(),
        P(),
        P("tensor", None),
        P(),
        P(),
        P(),
        P(None, "tensor"),
        P("tensor", None),
        P("tensor", None),
        P(),
        P("dp", ("seq", "tensor"), None),
    )
    out_specs = (
        P("dp", ("seq", "tensor"), None),
        P("dp", ("seq", "tensor"), None),
        P(("dp", "seq", "tensor")),
        P(("dp", "seq", "tensor")),
        P(("dp", "seq"), "tensor"),
        P("tensor", ("dp", "seq")),
        P(("dp", "seq", "tensor"), None),
        P(("dp", "seq", "tensor"), None),
        P(("dp", "seq", "tensor")),
        P("tensor", ("dp", "seq")),
        P(("dp", "seq", "tensor")),
        P(("dp", "seq", "tensor")),
        P(("dp", "seq", "tensor")),
        P(("dp", "seq"), "tensor"),
        P("tensor", ("dp", "seq")),
        P("tensor", ("dp", "seq")),
        P(("dp", "seq", "tensor")),
    )
    return jax.shard_map(
        on_device, mesh=mesh, in_specs=in_specs, out_specs=out_specs, check_vma=False
    )
```

```python
import functools

import jax
import jax.numpy as jnp
from jax import lax
from jax.experimental import pallas as pl
from jax.experimental.pallas import tpu as pltpu
from jax.sharding import PartitionSpec as P

epsilon = 1e-05
negative = -1e30
log2e = 1.4426950408889634
f32 = jnp.float32
low = jnp.bfloat16
vmem_bytes = 48 * 1024 * 1024


def dot(left, right):
    return jnp.dot(left, right, preferred_element_type=f32)


def contract_rows(left, right):
    return lax.dot_general(left, right, (((0,), (0,)), ((), ())), preferred_element_type=f32)


def contract_cols(left, right):
    return lax.dot_general(left, right, (((1,), (1,)), ((), ())), preferred_element_type=f32)


def allowed_mask(start, base, flip, pos_ref):
    offset = lax.broadcasted_iota(jnp.int32, (start, 1), 0)
    key_pos = base + (offset ^ flip)
    return (key_pos <= pos_ref[0:1, :]) & (key_pos >= pos_ref[1:2, :])


def over_blocks(info, body):
    body(0, True)
    lax.fori_loop(1, info[0], lambda s, c: (body(s, False), c)[1], 0)
    lax.fori_loop(info[0], info[1], lambda s, c: (body(s, True), c)[1], 0)


def gather_keys(near_ref, far_ref, head, places):
    rows = near_ref.shape[1]

    def one(s, carry):
        for side, ref in enumerate((near_ref, far_ref)):
            where = pl.multiple_of(s * 2 * rows + side * rows, rows)
            item = ref[s]
            for kind, target in enumerate(places):
                for turned, place in target:
                    part = item[:, kind * head : (kind + 1) * head]
                    if turned:
                        place[:, pl.ds(where, rows)] = part.T
                    else:
                        place[pl.ds(where, rows), :] = part
        return carry

    lax.fori_loop(0, near_ref.shape[0], one, 0)


def attend_kernel(
    scale,
    info,
    q_ref,
    near_ref,
    far_ref,
    pos_ref,
    o_ref,
    lse_ref,
    k_ref,
    vt_ref,
    m_ref,
    l_ref,
    acc_ref,
):
    span = q_ref.shape[0]
    head = k_ref.shape[1]
    pair = q_ref.shape[1] // head
    step = pl.program_id(0)

    @pl.when(step == 0)
    def _():
        gather_keys(near_ref, far_ref, head, [[(False, k_ref)], [(True, vt_ref)]])

    turned = [q_ref[:, h * head : (h + 1) * head].T for h in range(pair)]
    m_ref[...] = jnp.full_like(m_ref, negative)
    l_ref[...] = jnp.zeros_like(l_ref)
    acc_ref[...] = jnp.zeros_like(acc_ref)

    def body(s, masked):
        where = pl.multiple_of(s * span, span)
        key_block = k_ref[pl.ds(where, span), :]
        value_block = vt_ref[:, pl.ds(where, span)]
        if masked:
            allowed = allowed_mask(span, (info[2] - s) * span, info[3], pos_ref)
        for h in range(pair):
            scores = dot(key_block, turned[h]) * scale
            if masked:
                scores = jnp.where(allowed, scores, negative)
            before = m_ref[h]
            after = jnp.maximum(before, jnp.max(scores, axis=0, keepdims=True))
            weights = jnp.exp2(scores - after)
            shrink = jnp.exp2(before - after)
            m_ref[h] = after
            l_ref[h] = l_ref[h] * shrink + jnp.sum(weights, axis=0, keepdims=True)
            acc_ref[h] = acc_ref[h] * shrink + dot(value_block, weights.astype(low))

    over_blocks(info, body)
    for h in range(pair):
        total = l_ref[h]
        lse_ref[pl.ds(step * pair + h, 1), :] = m_ref[h] + jnp.log2(total)
        o_ref[:, h * head : (h + 1) * head] = (acc_ref[h] / total).T.astype(low)


def attend_back_kernel(
    scale,
    unit,
    info,
    q_ref,
    do_ref,
    o_ref,
    lse_ref,
    near_ref,
    far_ref,
    pos_ref,
    dq_ref,
    dkv_ref,
    k_ref,
    kt_ref,
    v_ref,
    dk_ref,
    dv_ref,
    dqt_ref,
):
    span = q_ref.shape[0]
    head = k_ref.shape[1]
    pair = q_ref.shape[1] // head
    step = pl.program_id(0)

    @pl.when(step == 0)
    def _():
        dk_ref[...] = jnp.zeros_like(dk_ref)
        dv_ref[...] = jnp.zeros_like(dv_ref)
        gather_keys(
            near_ref, far_ref, head, [[(False, k_ref), (True, kt_ref)], [(False, v_ref)]]
        )

    dqt_ref[...] = jnp.zeros_like(dqt_ref)
    queries = [q_ref[:, h * head : (h + 1) * head] for h in range(pair)]
    grads = [do_ref[:, h * head : (h + 1) * head] for h in range(pair)]
    queries_t = [item.T for item in queries]
    grads_t = [item.T for item in grads]
    inner = [
        jnp.sum(
            grads_t[h].astype(f32) * o_ref[:, h * head : (h + 1) * head].T.astype(f32),
            axis=0,
            keepdims=True,
        )
        for h in range(pair)
    ]
    totals = [lse_ref[pl.ds(step * pair + h, 1), :] for h in range(pair)]

    def body(s, masked):
        where = pl.multiple_of(s * span, span)
        key_block = k_ref[pl.ds(where, span), :]
        key_turned = kt_ref[:, pl.ds(where, span)]
        value_block = v_ref[pl.ds(where, span), :]
        if masked:
            allowed = allowed_mask(span, (info[2] - s) * span, info[3], pos_ref)
        key_part = jnp.zeros((span, head), f32)
        value_part = jnp.zeros((span, head), f32)
        for h in range(pair):
            scores = dot(key_block, queries_t[h]) * scale - totals[h]
            if masked:
                scores = jnp.where(allowed, scores, negative)
            probs = jnp.exp2(scores)
            grad_probs = dot(value_block, grads_t[h])
            grad_scores = (probs * (grad_probs - inner[h])).astype(low)
            key_part += dot(grad_scores, queries[h])
            value_part += dot(probs.astype(low), grads[h])
            dqt_ref[h] += dot(key_turned, grad_scores)
        dk_ref[pl.ds(where, span), :] += key_part
        dv_ref[pl.ds(where, span), :] += value_part

    over_blocks(info, body)
    for h in range(pair):
        dq_ref[:, h * head : (h + 1) * head] = (dqt_ref[h] * unit).T.astype(low)

    @pl.when(step == pl.num_programs(0) - 1)
    def _():
        dkv_ref[0] = (dk_ref[...] * unit).astype(low)
        dkv_ref[1] = dv_ref[...].astype(low)


def attend(info, query, near, far, pos, heads, head):
    span = query.shape[0]
    window = near.shape[0] * span
    pair = 2
    scale = head**-0.5 * log2e
    work = heads * span * window * head
    piece = pl.BlockSpec(near.shape, lambda i, s: (0, 0, 0))
    spec = pltpu.PrefetchScalarGridSpec(
        num_scalar_prefetch=1,
        grid=(heads // pair,),
        in_specs=[
            pl.BlockSpec((span, pair * head), lambda i, s: (0, i)),
            piece,
            piece,
            pl.BlockSpec(pos.shape, lambda i, s: (0, 0)),
        ],
        out_specs=[
            pl.BlockSpec((span, pair * head), lambda i, s: (0, i)),
            pl.BlockSpec((heads, span), lambda i, s: (0, 0)),
        ],
        scratch_shapes=[
            pltpu.VMEM((window, head), low),
            pltpu.VMEM((head, window), low),
            pltpu.VMEM((pair, 1, span), f32),
            pltpu.VMEM((pair, 1, span), f32),
            pltpu.VMEM((pair, head, span), f32),
        ],
    )
    return pl.pallas_call(
        functools.partial(attend_kernel, scale),
        grid_spec=spec,
        out_shape=(
            jax.ShapeDtypeStruct(query.shape, low),
            jax.ShapeDtypeStruct((heads, span), f32),
        ),
        compiler_params=pltpu.CompilerParams(vmem_limit_bytes=vmem_bytes),
        cost_estimate=pl.CostEstimate(
            flops=8 * work, bytes_accessed=4 * query.size, transcendentals=work // head
        ),
        name="attend",
    )(info, query, near, far, pos)


def attend_back(info, query, grad, attended, lse, near, far, pos, heads, head):
    span = query.shape[0]
    window = near.shape[0] * span
    pair = 2
    scale = head**-0.5 * log2e
    work = heads * span * window * head
    wide = pl.BlockSpec((span, pair * head), lambda i, s: (0, i))
    piece = pl.BlockSpec(near.shape, lambda i, s: (0, 0, 0))
    spec = pltpu.PrefetchScalarGridSpec(
        num_scalar_prefetch=1,
        grid=(heads // pair,),
        in_specs=[
            wide,
            wide,
            wide,
            pl.BlockSpec((heads, span), lambda i, s: (0, 0)),
            piece,
            piece,
            pl.BlockSpec(pos.shape, lambda i, s: (0, 0)),
        ],
        out_specs=[wide, pl.BlockSpec((2, window, head), lambda i, s: (0, 0, 0))],
        scratch_shapes=[
            pltpu.VMEM((window, head), low),
            pltpu.VMEM((head, window), low),
            pltpu.VMEM((window, head), low),
            pltpu.VMEM((window, head), f32),
            pltpu.VMEM((window, head), f32),
            pltpu.VMEM((pair, head, span), f32),
        ],
    )
    return pl.pallas_call(
        functools.partial(attend_back_kernel, scale, head**-0.5),
        grid_spec=spec,
        out_shape=(
            jax.ShapeDtypeStruct(query.shape, low),
            jax.ShapeDtypeStruct((2, window, head), low),
        ),
        compiler_params=pltpu.CompilerParams(vmem_limit_bytes=vmem_bytes),
        cost_estimate=pl.CostEstimate(
            flops=20 * work, bytes_accessed=8 * query.size, transcendentals=work // head
        ),
        name="attend_back",
    )(info, query, grad, attended, lse, near, far, pos)


def gelu_both(value, grad):
    inside = 0.7978845608028654 * (value + 0.044715 * value * value * value)
    bend = jnp.tanh(inside)
    half = 0.5 * (1.0 + bend)
    slope = half + 0.5 * value * (1.0 - bend * bend) * 0.7978845608028654 * (
        1.0 + 3.0 * 0.044715 * value * value
    )
    return (value * half).astype(low), (grad.astype(f32) * slope).astype(low)


def up_kernel(near_ref, far_ref, w_ref, b_ref, g_ref, act_ref, gh_ref, sum_ref, x_ref):
    rows = near_ref.shape[0]

    @pl.when(pl.program_id(0) == 0)
    def _():
        x_ref[:rows] = near_ref[...]
        x_ref[rows:] = far_ref[...]

    tile = min(256, w_ref.shape[1])
    for at in range(0, w_ref.shape[1], tile):
        cut = slice(at, at + tile)
        hidden = dot(x_ref[...], w_ref[:, cut]) + b_ref[:, cut]
        act, grad = gelu_both(hidden, g_ref[:, cut])
        act_ref[:, cut] = act
        gh_ref[:, cut] = grad
        sum_ref[:, cut] = jnp.sum(grad.astype(f32), axis=0, keepdims=True)


def up(near, far, w_up, bias, grad_act):
    rows, width = near.shape
    units = w_up.shape[1]
    tile = min(512, units)
    row = pl.BlockSpec((rows, width), lambda i: (0, 0))
    tall = pl.BlockSpec((2 * rows, tile), lambda i: (0, i))
    thin = pl.BlockSpec((1, tile), lambda i: (0, i))
    shape = jax.ShapeDtypeStruct((2 * rows, units), low)
    return pl.pallas_call(
        up_kernel,
        grid=(units // tile,),
        in_specs=[row, row, pl.BlockSpec((width, tile), lambda i: (0, i)), thin, tall],
        out_specs=[tall, tall, thin],
        out_shape=(shape, shape, jax.ShapeDtypeStruct((1, units), f32)),
        scratch_shapes=[pltpu.VMEM((2 * rows, width), low)],
        compiler_params=pltpu.CompilerParams(vmem_limit_bytes=vmem_bytes),
        cost_estimate=pl.CostEstimate(
            flops=4 * rows * width * units,
            bytes_accessed=2 * width * units + 16 * rows * units,
            transcendentals=2 * rows * units,
        ),
        name="up",
    )(near, far, w_up, bias.reshape(1, -1), grad_act)


def share_kernel(
    at, near_ref, far_ref, gnear_ref, gfar_ref, up_ref, down_ref, b_ref, act_ref, gh_ref, x_ref, g_ref
):
    rows = near_ref.shape[0]

    @pl.when(pl.program_id(0) == 0)
    def _():
        x_ref[:rows] = near_ref[...]
        x_ref[rows:] = far_ref[...]
        g_ref[:rows] = gnear_ref[...]
        g_ref[rows:] = gfar_ref[...]

    tile = min(256, up_ref.shape[1])
    for start in range(0, up_ref.shape[1], tile):
        cut = slice(start, start + tile)
        hidden = dot(x_ref[...], up_ref[:, cut]) + b_ref[:, cut]
        grad_act = contract_cols(g_ref[...], down_ref[cut, :])
        act, grad = gelu_both(hidden, grad_act)
        act_ref[:, cut] = act
        gh_ref[:, cut] = grad


def share(at, near, far, grad_near, grad_far, w_up, w_down, bias, units):
    rows, width = near.shape
    tile = min(512, units)
    tiles = units // tile
    row = pl.BlockSpec((rows, width), lambda i, s: (0, 0))
    tall = pl.BlockSpec((2 * rows, tile), lambda i, s: (0, i))
    shape = jax.ShapeDtypeStruct((2 * rows, units), low)
    spec = pltpu.PrefetchScalarGridSpec(
        num_scalar_prefetch=1,
        grid=(tiles,),
        in_specs=[
            row,
            row,
            row,
            row,
            pl.BlockSpec((width, tile), lambda i, s: (0, s[0] * tiles + i)),
            pl.BlockSpec((tile, width), lambda i, s: (s[0] * tiles + i, 0)),
            pl.BlockSpec((1, tile), lambda i, s: (0, s[0] * tiles + i)),
        ],
        out_specs=[tall, tall],
        scratch_shapes=[pltpu.VMEM((2 * rows, width), low)] * 2,
    )
    return pl.pallas_call(
        share_kernel,
        grid_spec=spec,
        out_shape=(shape, shape),
        compiler_params=pltpu.CompilerParams(vmem_limit_bytes=vmem_bytes),
        cost_estimate=pl.CostEstimate(
            flops=8 * rows * width * units,
            bytes_accessed=4 * width * units + 8 * rows * (units + width),
            transcendentals=2 * rows * units,
        ),
        name="share",
    )(at, near, far, grad_near, grad_far, w_up, w_down, bias.reshape(1, -1))


turns = ((3, 0), (1, 0), (3, 1), (2, 1), (1, 1), (2, 0), (0, 0), (0, 1))


def joined(items, place):
    if len(items) == 1:
        return items[0][...]
    start = 0
    for item in items:
        place[start : start + item.shape[0]] = item[...]
        start += item.shape[0]
    return place[...]


def store_turn(turn, result, outs):
    for index, out in enumerate(outs):

        @pl.when(turn // 2 == index)
        def _(out=out):
            out[0] = result.astype(out.dtype)


def hidden_kernel(lefts, at, *refs):
    left_refs, right_refs = refs[:lefts], refs[lefts:-6]
    outs, (left_place, right_place) = refs[-6:-2], refs[-2:]
    left = joined(left_refs, left_place)
    right = joined(right_refs, right_place)
    store_turn(pl.program_id(0), contract_rows(left, right), outs)


def hidden_weights(at, lefts, pieces, units, part, name):
    total = len(turns)
    span = lefts[0].shape[0]
    rows = span // 2
    half = units // 2
    depth = len(lefts) * span

    def left_of(own):
        def place(i, s):
            return (0, s[2 * total] * 2 + s[total + i] if own else s[total + i])

        return pl.BlockSpec((span, half), place)

    def out_of(index):
        return pl.BlockSpec((1, half, part), lambda i, s: (jnp.clip(i - 2 * index, 0, 1), 0, 0))

    spec = pltpu.PrefetchScalarGridSpec(
        num_scalar_prefetch=1,
        grid=(total,),
        in_specs=[left_of(n == 0) for n in range(len(lefts))]
        + [pl.BlockSpec((rows, part), lambda i, s: (0, s[i])) for _ in pieces],
        out_specs=[out_of(index) for index in range(4)],
        scratch_shapes=[pltpu.VMEM((depth, half), low), pltpu.VMEM((depth, part), low)],
    )
    return pl.pallas_call(
        functools.partial(hidden_kernel, len(lefts)),
        grid_spec=spec,
        out_shape=tuple(jax.ShapeDtypeStruct((2, half, part), low) for _ in range(4)),
        compiler_params=pltpu.CompilerParams(vmem_limit_bytes=60 * 1024 * 1024),
        cost_estimate=pl.CostEstimate(
            flops=2 * total * depth * half * part,
            bytes_accessed=4 * depth * (units + 4 * part),
            transcendentals=0,
        ),
        name=name,
    )(at, *lefts, *pieces)


def place_kernel(count, at, *refs):
    parts, (down_ref, up_ref) = refs[: 2 * count], refs[2 * count :]
    for step in range(count):

        @pl.when(pl.program_id(0) == step)
        def _(step=step):
            down_ref[...] = parts[step][0].astype(f32)
            up_ref[...] = parts[count + step][0].astype(f32).T


def place(at, downs, ups):
    count = len(downs)
    _, units, part = downs[0].shape
    piece = pl.BlockSpec((1, units, part), lambda i, s: (0, 0, 0))
    spec = pltpu.PrefetchScalarGridSpec(
        num_scalar_prefetch=1,
        grid=(count,),
        in_specs=[piece] * (2 * count),
        out_specs=[
            pl.BlockSpec((units, part), lambda i, s: (lax.rem(s[0] - i + count, count), 0)),
            pl.BlockSpec((part, units), lambda i, s: (0, lax.rem(s[0] - i + count, count))),
        ],
    )
    return pl.pallas_call(
        functools.partial(place_kernel, count),
        grid_spec=spec,
        out_shape=(
            jax.ShapeDtypeStruct((count * units, part), f32),
            jax.ShapeDtypeStruct((part, count * units), f32),
        ),
        compiler_params=pltpu.CompilerParams(vmem_limit_bytes=vmem_bytes),
        cost_estimate=pl.CostEstimate(
            flops=0, bytes_accessed=12 * count * units * part, transcendentals=0
        ),
        name="place",
    )(at, *downs, *ups)


def branch_kernel(at, near_ref, far_ref, y_ref, *refs):
    outs, place = refs[:4], refs[4]
    result = contract_rows(joined((near_ref, far_ref), place), y_ref[...])
    store_turn(pl.program_id(0), result, outs)


def branch_weights(at, near, far, right, part, name):
    total = len(turns)
    rows = near.shape[0]
    half = part // 2
    wide = right.shape[1]
    piece = pl.BlockSpec((rows, half), lambda i, s: (0, s[i] * 2 + s[total + i]))

    def all_of(item):
        return pl.BlockSpec(item.shape, lambda i, s: (0, 0))

    def out_of(index):
        return pl.BlockSpec((1, half, wide), lambda i, s: (jnp.clip(i - 2 * index, 0, 1), 0, 0))

    spec = pltpu.PrefetchScalarGridSpec(
        num_scalar_prefetch=1,
        grid=(total,),
        in_specs=[piece, piece, all_of(right)],
        out_specs=[out_of(index) for index in range(4)],
        scratch_shapes=[pltpu.VMEM((2 * rows, half), low)],
    )
    return pl.pallas_call(
        branch_kernel,
        grid_spec=spec,
        out_shape=tuple(jax.ShapeDtypeStruct((2, half, wide), low) for _ in range(4)),
        compiler_params=pltpu.CompilerParams(vmem_limit_bytes=vmem_bytes),
        cost_estimate=pl.CostEstimate(
            flops=4 * total * rows * half * wide,
            bytes_accessed=2 * total * half * wide,
            transcendentals=0,
        ),
        name=name,
    )(at, near, far, right)


def swap(item):
    return lax.ppermute(item, "tensor", [(0, 1), (1, 0)])


def cross(item, bits):
    size = lax.axis_size("dp")
    return lax.ppermute(item, "dp", [(i, i ^ bits) for i in range(size)])


def shift(item, by):
    size = lax.axis_size("seq")
    return lax.ppermute(item, "seq", [(i, (i + by) % size) for i in range(size)])


def shift_up(item, by):
    size = lax.axis_size("seq")
    return lax.ppermute(item, "seq", [(i, i + by) for i in range(size - by)])


def shift_down(item, by):
    size = lax.axis_size("seq")
    return lax.ppermute(item, "seq", [(i + by, i) for i in range(size - by)])


def pair_gather(item):
    return jnp.concatenate([item, swap(item)], axis=0)


def after(item, *others):
    return lax.optimization_barrier((item, *others))


def pair_sum(both):
    half = both.shape[0] // 2
    return both[:half].astype(f32) + swap(both[half:]).astype(f32)


def dp_first(parts, size):
    send_x, send_y, kept, own = (item.reshape(2, size, *item.shape[1:]) for item in parts)
    got_x = cross(send_x, 1)
    got_y = cross(send_y, 2)
    second_a = (kept[1].astype(f32) + got_x[0].astype(f32)).astype(low)
    second_b = (kept[0].astype(f32) + got_y[0].astype(f32)).astype(low)
    return second_a, second_b, own, got_x, got_y


def dp_last(second_a, second_b, own, got_x, got_y):
    last_a = cross(second_a, 2)
    last_b = cross(second_b, 1)
    return jnp.concatenate(
        [
            own[0].astype(f32) + got_x[1].astype(f32) + last_a.astype(f32),
            own[1].astype(f32) + got_y[1].astype(f32) + last_b.astype(f32),
        ],
        axis=1,
    )


def norm_parts(rows):
    centre = rows - jnp.mean(rows, axis=-1, keepdims=True)
    inverse = lax.rsqrt(jnp.mean(centre * centre, axis=-1, keepdims=True) + epsilon)
    return centre * inverse, inverse


def norm_back(grad, unit, inverse, gain):
    scaled = grad * gain
    part = (
        scaled
        - jnp.mean(scaled, axis=-1, keepdims=True)
        - unit * jnp.mean(scaled * unit, axis=-1, keepdims=True)
    )
    return part * inverse, jnp.sum(grad * unit, axis=0), jnp.sum(grad, axis=0)


def on_device(
    tokens,
    lengths,
    ln1_gain,
    ln1_bias,
    w_query,
    b_query,
    w_key,
    w_value,
    b_value,
    w_out,
    b_out,
    ln2_gain,
    ln2_bias,
    w_up,
    b_up,
    w_down,
    b_down,
    cotangent,
):
    shard = tokens[0].astype(f32)
    rows_own, width = shard.shape
    seqs = lax.axis_size("seq")
    dps = lax.axis_size("dp")
    span = 2 * rows_own
    heads, head = b_query.shape
    at_dp, at_seq, at_core = (lax.axis_index(name) for name in ("dp", "seq", "tensor"))
    flip = at_core * rows_own
    span_start = at_seq * span
    hidden_local = w_up.shape[1]
    hidden_part = hidden_local // seqs
    dp_part = width // dps
    out_part = dp_part // seqs

    ends = jnp.cumsum(lengths[0], dtype=jnp.int32)
    row_pos = span_start + (jnp.arange(span, dtype=jnp.int32) ^ flip)
    row_start = jnp.max(
        jnp.where(row_pos[:, None] >= ends[None, :], ends[None, :], 0), axis=1
    ).astype(jnp.int32)
    pos = jnp.zeros((8, span), jnp.int32).at[0].set(row_pos).at[1].set(row_start)
    first, last = jnp.min(row_start), jnp.max(row_start)
    whole_to = jnp.clip(at_seq + 1 - (last + span - 1) // span, 1, at_seq + 1)
    some_to = jnp.clip(at_seq + 1 - first // span, whole_to, at_seq + 1)
    info = jnp.stack([whole_to, some_to, at_seq, flip]).astype(jnp.int32)

    unit_one, inverse_one = norm_parts(shard)
    normed = (unit_one * ln1_gain + ln1_bias).astype(low)
    w_both = jnp.concatenate([w_key, w_value], axis=1)
    b_both = jnp.concatenate([jnp.zeros_like(b_value), b_value])
    both_own = (dot(normed, w_both) + b_both).astype(low)
    pieces = [shift_up(both_own, by) for by in range(1, seqs)]
    grad_own = cotangent[0]
    grad_own, both_own = after(grad_own, both_own)
    grad_held = [grad_own]
    for step in range(1, seqs):
        grad_held.append(shift(grad_held[-1], 1))
    grad_far = [swap(grad_own)]
    grad_act = contract_cols(jnp.concatenate([grad_own, grad_far[0]], axis=0), w_down).astype(low)
    grad_act, *pieces = after(grad_act, *pieces)
    near = jnp.stack([both_own] + pieces)
    far = swap(near)
    normed_far = swap(normed)
    normed_all = jnp.concatenate([normed, normed_far], axis=0)
    query = (dot(normed_all, w_query) + b_query.reshape(-1)).astype(low)

    if seqs > 1:
        query, grad_held[1] = after(query, grad_held[1])
    attended, lse = attend(info, query, near, far, pos, heads, head)
    if seqs > 2:
        attended, grad_held[2] = after(attended, grad_held[2])
    middle = shard + (pair_sum(dot(attended, w_out).astype(low)) + b_out)
    unit_two, inverse_two = norm_parts(middle)
    normed_two = (unit_two * ln2_gain + ln2_bias).astype(low)

    held = [normed_two]
    for step in range(1, seqs):
        held.append(shift(held[-1], 1))
    held_far = [swap(normed_two)]
    activated, grad_hidden, grad_b_up = up(held[0], held_far[0], w_up, b_up, grad_act)
    if seqs > 3:
        grad_hidden, grad_held[3] = after(grad_hidden, grad_held[3])
    grad_normed_two = contract_cols(grad_hidden, w_up).astype(low)
    if seqs > 1:
        grad_normed_two, held[1] = after(grad_normed_two, held[1])
    grad_normed_two = pair_sum(grad_normed_two)

    back, grad_ln2_gain, grad_ln2_bias = norm_back(
        grad_normed_two, unit_two, inverse_two, ln2_gain
    )
    grad_out = grad_own.astype(f32)
    grad_b_down = jnp.sum(grad_out, axis=0)
    grad_middle = grad_out + back
    grad_branch = grad_middle.astype(low)
    grad_b_out = jnp.sum(grad_branch.astype(f32), axis=0)
    grad_branch_far = swap(grad_branch)
    grad_branch_all = jnp.concatenate([grad_branch, grad_branch_far], axis=0)
    grad_attended = contract_cols(grad_branch_all, w_out).astype(low)
    blocks = [at_dp ^ r for r, _ in turns]
    halves = [jnp.int32(half) for _, half in turns]
    table = jnp.stack(blocks + halves + [at_seq, at_core]).astype(jnp.int32)

    parts_out = branch_weights(
        table, grad_branch, grad_branch_far, attended, dp_part, "weight_out"
    )

    share_at = at_seq.reshape(1).astype(jnp.int32)
    acts, grads = [activated], [grad_hidden]

    def shared_part(step):
        held_far.append(swap(held[step]))
        grad_far.append(swap(grad_held[step]))
        act, grad = share(
            share_at,
            held[step],
            held_far[step],
            grad_held[step],
            grad_far[step],
            w_up,
            w_down,
            b_up,
            hidden_part,
        )
        acts.append(act)
        grads.append(grad)

    if seqs > 2:
        shared_part(1)
        grad_attended, acts[1], held[2], *parts_out = after(
            grad_attended, acts[1], held[2], *parts_out
        )
    first_out = dp_first(parts_out, 1)

    grad_query, grad_both = attend_back(
        info, query, grad_attended, attended, lse, near, far, pos, heads, head
    )
    if seqs > 1:
        grad_both, held[-1], *seconds = after(grad_both, held[-1], *first_out[:2])
        first_out = (*seconds, *first_out[2:])
    grad_both = grad_both.reshape(2, seqs, 2, rows_own, head)
    kept = lax.dynamic_index_in_dim(grad_both, at_core, 0, False)
    given = lax.dynamic_index_in_dim(grad_both, 1 - at_core, 0, False)
    grad_kv = (kept.astype(f32) + swap(given)[:, ::-1].astype(f32)).astype(low)
    grad_kv = grad_kv.reshape(seqs, span, head)
    total = grad_kv[0].astype(f32)
    for by in range(1, seqs):
        total = total + shift_down(grad_kv[by], by).astype(f32)
    grad_kv = total.astype(low)
    grad_qkv = jnp.concatenate([grad_query, grad_kv], axis=1)
    w_qkv = jnp.concatenate([w_query, jnp.where(at_core == 0, w_key, w_value)], axis=1)
    grad_normed = pair_sum(contract_cols(grad_qkv, w_qkv).astype(low))
    back, grad_ln1_gain, grad_ln1_bias = norm_back(
        grad_normed, unit_one, inverse_one, ln1_gain
    )
    grad_input = (grad_middle + back).astype(low)[None]

    parts = branch_weights(table, normed, normed_far, grad_qkv, dp_part, "weight_query")
    grad_b_value = jnp.where(at_core == 1, jnp.sum(grad_kv.astype(f32), axis=0), 0.0)
    grad_b_query = jnp.sum(grad_query.astype(f32), axis=0)
    features = [
        grad_ln1_gain,
        grad_ln1_bias,
        grad_b_out,
        grad_ln2_gain,
        grad_ln2_bias,
        grad_b_down,
    ]
    count = len(features)
    features = jnp.concatenate([item.reshape(-1, head) for item in features], axis=0)
    rows = features.shape[0]
    features = features + swap(features)
    values = grad_b_value.reshape(1, head)
    values = values + swap(values)
    packed = jnp.concatenate(
        [
            features,
            grad_b_up.reshape(-1, head),
            grad_b_query.reshape(-1, head),
            jnp.broadcast_to(values, (8, head)),
        ],
        axis=0,
    )
    share_at, packed, *parts = after(share_at, packed, *parts)
    first_query = dp_first(parts, 1)
    total = packed + cross(packed, 1) + cross(packed, 2) + cross(packed, 3)

    for step in range(len(acts), seqs):
        shared_part(step)
    acts[-1], total, *seconds = after(acts[-1], total, *first_query[:2])
    first_query = (*seconds, *first_query[2:])
    downs = hidden_weights(
        table,
        acts,
        [item for couple in zip(grad_held, grad_far) for item in couple],
        hidden_part,
        dp_part,
        "weight_down",
    )
    sum_branch = jnp.concatenate([dp_last(*first_out)[0], dp_last(*first_query)[0]], axis=1)
    grads[0], sum_branch, *downs = after(grads[0], sum_branch, *downs)
    first_down = dp_first(downs, 1)
    packed = total
    for by in range(1, seqs):
        total = total + shift(packed, by)
    ups = hidden_weights(
        table,
        grads,
        [item for couple in zip(held, held_far) for item in couple],
        hidden_part,
        dp_part,
        "weight_up",
    )
    activated, *ups = after(activated, *ups)
    first_up = dp_first(ups, 1)
    activated, *seconds = after(activated, *first_down[:2])
    first_down = (*seconds, *first_down[2:])
    result = dot(activated, w_down).astype(low)
    sum_down = dp_last(*first_down).astype(low)
    result, sum_down, *seconds = after(result, sum_down, *first_up[:2])
    first_up = (*seconds, *first_up[2:])
    output = (middle + (pair_sum(result) + b_down)).astype(low)[None]
    sum_up = dp_last(*first_up).astype(low)

    def to_seq(item, by, axis):
        at = lax.rem(at_seq + by, seqs)
        return lax.dynamic_slice_in_dim(item, at * out_part, out_part, axis)

    downs, ups = [], []
    for items, whole in ((downs, sum_down), (ups, sum_up)):
        items.append(to_seq(whole, 0, 2))
        for by in range(1, seqs):
            items.append(shift(to_seq(whole, by, 2), by))
    out_w_down, out_w_up = place(share_at, downs, ups)

    narrow = sum_branch.astype(low)
    branch = to_seq(sum_branch, 0, 0)
    for by in range(1, seqs):
        branch = branch + shift(to_seq(narrow, by, 0), by).astype(f32)
    out_w_out = branch[:, : heads * head].T
    out_qkv = branch[:, heads * head :]
    out_w_query = out_qkv[:, : heads * head]
    half = out_part // 2
    last_kv = out_qkv[:, heads * head :]
    mine = lax.dynamic_slice_in_dim(last_kv, at_core * half, half, 0)
    other = swap(lax.dynamic_slice_in_dim(last_kv, (1 - at_core) * half, half, 0))
    out_w_key = jnp.where(at_core == 0, mine, other)
    out_w_value = jnp.where(at_core == 0, other, mine)

    place_own = at_dp * seqs + at_seq

    def own_part(item, size, index):
        return lax.dynamic_slice_in_dim(item, index * size, size, item.ndim - 1)

    vectors = own_part(
        total[:rows].reshape(count, width), out_part // 2, place_own * 2 + at_core
    )
    thin = head // (dps * seqs)
    up_rows = b_up.shape[0]
    sum_b_up = own_part(total[rows : rows + up_rows], thin, place_own)
    sum_b_query = own_part(total[rows + up_rows : rows + up_rows + heads], thin, place_own)
    sum_b_value = own_part(total[rows + up_rows + heads], thin // 2, place_own * 2 + at_core)
    return (
        output,
        grad_input,
        vectors[0],
        vectors[1],
        out_w_query,
        sum_b_query,
        out_w_key,
        out_w_value,
        sum_b_value,
        out_w_out,
        vectors[2],
        vectors[3],
        vectors[4],
        out_w_up,
        sum_b_up,
        out_w_down,
        vectors[5],
    )


def solution(mesh):
    in_specs = (
        P("dp", ("seq", "tensor"), None),
        P("dp", None),
        P(),
        P(),
        P(None, "tensor"),
        P("tensor", None),
        P(),
        P(),
        P(),
        P("tensor", None),
        P(),
        P(),
        P(),
        P(None, "tensor"),
        P("tensor", None),
        P("tensor", None),
        P(),
        P("dp", ("seq", "tensor"), None),
    )
    out_specs = (
        P("dp", ("seq", "tensor"), None),
        P("dp", ("seq", "tensor"), None),
        P(("dp", "seq", "tensor")),
        P(("dp", "seq", "tensor")),
        P(("dp", "seq"), "tensor"),
        P("tensor", ("dp", "seq")),
        P(("dp", "seq", "tensor"), None),
        P(("dp", "seq", "tensor"), None),
        P(("dp", "seq", "tensor")),
        P("tensor", ("dp", "seq")),
        P(("dp", "seq", "tensor")),
        P(("dp", "seq", "tensor")),
        P(("dp", "seq", "tensor")),
        P(("dp", "seq"), "tensor"),
        P("tensor", ("dp", "seq")),
        P("tensor", ("dp", "seq")),
        P(("dp", "seq", "tensor")),
    )
    return jax.shard_map(
        on_device, mesh=mesh, in_specs=in_specs, out_specs=out_specs, check_vma=False
    )
```

```python
import functools

import jax
import jax.numpy as jnp
from jax import lax
from jax.experimental import pallas as pl
from jax.experimental.pallas import tpu as pltpu
from jax.sharding import PartitionSpec as P

epsilon = 1e-05
negative = -1e30
log2e = 1.4426950408889634
f32 = jnp.float32
low = jnp.bfloat16
vmem_bytes = 48 * 1024 * 1024


def dot(left, right):
    return jnp.dot(left, right, preferred_element_type=f32)


def contract_rows(left, right):
    return lax.dot_general(left, right, (((0,), (0,)), ((), ())), preferred_element_type=f32)


def contract_cols(left, right):
    return lax.dot_general(left, right, (((1,), (1,)), ((), ())), preferred_element_type=f32)


def allowed_mask(start, base, flip, pos_ref):
    offset = lax.broadcasted_iota(jnp.int32, (start, 1), 0)
    key_pos = base + (offset ^ flip)
    return (key_pos <= pos_ref[0:1, :]) & (key_pos >= pos_ref[1:2, :])


def over_blocks(info, body):
    body(0, True)
    lax.fori_loop(1, info[0], lambda s, c: (body(s, False), c)[1], 0)
    lax.fori_loop(info[0], info[1], lambda s, c: (body(s, True), c)[1], 0)


def gather_keys(near_ref, far_ref, head, places):
    rows = near_ref.shape[1]

    def one(s, carry):
        for side, ref in enumerate((near_ref, far_ref)):
            where = pl.multiple_of(s * 2 * rows + side * rows, rows)
            item = ref[s]
            for kind, target in enumerate(places):
                for turned, place in target:
                    part = item[:, kind * head : (kind + 1) * head]
                    if turned:
                        place[:, pl.ds(where, rows)] = part.T
                    else:
                        place[pl.ds(where, rows), :] = part
        return carry

    lax.fori_loop(0, near_ref.shape[0], one, 0)


def attend_kernel(
    scale,
    info,
    q_ref,
    near_ref,
    far_ref,
    pos_ref,
    o_ref,
    lse_ref,
    k_ref,
    vt_ref,
    m_ref,
    l_ref,
    acc_ref,
):
    span = q_ref.shape[0]
    head = k_ref.shape[1]
    pair = q_ref.shape[1] // head
    step = pl.program_id(0)

    @pl.when(step == 0)
    def _():
        gather_keys(near_ref, far_ref, head, [[(False, k_ref)], [(True, vt_ref)]])

    turned = [q_ref[:, h * head : (h + 1) * head].T for h in range(pair)]
    m_ref[...] = jnp.full_like(m_ref, negative)
    l_ref[...] = jnp.zeros_like(l_ref)
    acc_ref[...] = jnp.zeros_like(acc_ref)

    def body(s, masked):
        where = pl.multiple_of(s * span, span)
        key_block = k_ref[pl.ds(where, span), :]
        value_block = vt_ref[:, pl.ds(where, span)]
        if masked:
            allowed = allowed_mask(span, (info[2] - s) * span, info[3], pos_ref)
        for h in range(pair):
            scores = dot(key_block, turned[h]) * scale
            if masked:
                scores = jnp.where(allowed, scores, negative)
            before = m_ref[h]
            after = jnp.maximum(before, jnp.max(scores, axis=0, keepdims=True))
            weights = jnp.exp2(scores - after)
            shrink = jnp.exp2(before - after)
            m_ref[h] = after
            l_ref[h] = l_ref[h] * shrink + jnp.sum(weights, axis=0, keepdims=True)
            acc_ref[h] = acc_ref[h] * shrink + dot(value_block, weights.astype(low))

    over_blocks(info, body)
    for h in range(pair):
        total = l_ref[h]
        lse_ref[pl.ds(step * pair + h, 1), :] = m_ref[h] + jnp.log2(total)
        o_ref[:, h * head : (h + 1) * head] = (acc_ref[h] / total).T.astype(low)


def attend_back_kernel(
    scale,
    unit,
    info,
    q_ref,
    do_ref,
    o_ref,
    lse_ref,
    near_ref,
    far_ref,
    pos_ref,
    dq_ref,
    dkv_ref,
    k_ref,
    kt_ref,
    v_ref,
    dk_ref,
    dv_ref,
    dqt_ref,
):
    span = q_ref.shape[0]
    head = k_ref.shape[1]
    pair = q_ref.shape[1] // head
    step = pl.program_id(0)

    @pl.when(step == 0)
    def _():
        dk_ref[...] = jnp.zeros_like(dk_ref)
        dv_ref[...] = jnp.zeros_like(dv_ref)
        gather_keys(
            near_ref, far_ref, head, [[(False, k_ref), (True, kt_ref)], [(False, v_ref)]]
        )

    dqt_ref[...] = jnp.zeros_like(dqt_ref)
    queries = [q_ref[:, h * head : (h + 1) * head] for h in range(pair)]
    grads = [do_ref[:, h * head : (h + 1) * head] for h in range(pair)]
    queries_t = [item.T for item in queries]
    grads_t = [item.T for item in grads]
    inner = [
        jnp.sum(
            grads_t[h].astype(f32) * o_ref[:, h * head : (h + 1) * head].T.astype(f32),
            axis=0,
            keepdims=True,
        )
        for h in range(pair)
    ]
    totals = [lse_ref[pl.ds(step * pair + h, 1), :] for h in range(pair)]

    def body(s, masked):
        where = pl.multiple_of(s * span, span)
        key_block = k_ref[pl.ds(where, span), :]
        key_turned = kt_ref[:, pl.ds(where, span)]
        value_block = v_ref[pl.ds(where, span), :]
        if masked:
            allowed = allowed_mask(span, (info[2] - s) * span, info[3], pos_ref)
        key_part = jnp.zeros((span, head), f32)
        value_part = jnp.zeros((span, head), f32)
        for h in range(pair):
            scores = dot(key_block, queries_t[h]) * scale - totals[h]
            if masked:
                scores = jnp.where(allowed, scores, negative)
            probs = jnp.exp2(scores)
            grad_probs = dot(value_block, grads_t[h])
            grad_scores = (probs * (grad_probs - inner[h])).astype(low)
            key_part += dot(grad_scores, queries[h])
            value_part += dot(probs.astype(low), grads[h])
            dqt_ref[h] += dot(key_turned, grad_scores)
        dk_ref[pl.ds(where, span), :] += key_part
        dv_ref[pl.ds(where, span), :] += value_part

    over_blocks(info, body)
    for h in range(pair):
        dq_ref[:, h * head : (h + 1) * head] = (dqt_ref[h] * unit).T.astype(low)

    @pl.when(step == pl.num_programs(0) - 1)
    def _():
        dkv_ref[0] = (dk_ref[...] * unit).astype(low)
        dkv_ref[1] = dv_ref[...].astype(low)


def attend(info, query, near, far, pos, heads, head):
    span = query.shape[0]
    window = near.shape[0] * span
    pair = 2
    scale = head**-0.5 * log2e
    work = heads * span * window * head
    piece = pl.BlockSpec(near.shape, lambda i, s: (0, 0, 0))
    spec = pltpu.PrefetchScalarGridSpec(
        num_scalar_prefetch=1,
        grid=(heads // pair,),
        in_specs=[
            pl.BlockSpec((span, pair * head), lambda i, s: (0, i)),
            piece,
            piece,
            pl.BlockSpec(pos.shape, lambda i, s: (0, 0)),
        ],
        out_specs=[
            pl.BlockSpec((span, pair * head), lambda i, s: (0, i)),
            pl.BlockSpec((heads, span), lambda i, s: (0, 0)),
        ],
        scratch_shapes=[
            pltpu.VMEM((window, head), low),
            pltpu.VMEM((head, window), low),
            pltpu.VMEM((pair, 1, span), f32),
            pltpu.VMEM((pair, 1, span), f32),
            pltpu.VMEM((pair, head, span), f32),
        ],
    )
    return pl.pallas_call(
        functools.partial(attend_kernel, scale),
        grid_spec=spec,
        out_shape=(
            jax.ShapeDtypeStruct(query.shape, low),
            jax.ShapeDtypeStruct((heads, span), f32),
        ),
        compiler_params=pltpu.CompilerParams(vmem_limit_bytes=vmem_bytes),
        cost_estimate=pl.CostEstimate(
            flops=8 * work, bytes_accessed=4 * query.size, transcendentals=work // head
        ),
        name="attend",
    )(info, query, near, far, pos)


def attend_back(info, query, grad, attended, lse, near, far, pos, heads, head):
    span = query.shape[0]
    window = near.shape[0] * span
    pair = 2
    scale = head**-0.5 * log2e
    work = heads * span * window * head
    wide = pl.BlockSpec((span, pair * head), lambda i, s: (0, i))
    piece = pl.BlockSpec(near.shape, lambda i, s: (0, 0, 0))
    spec = pltpu.PrefetchScalarGridSpec(
        num_scalar_prefetch=1,
        grid=(heads // pair,),
        in_specs=[
            wide,
            wide,
            wide,
            pl.BlockSpec((heads, span), lambda i, s: (0, 0)),
            piece,
            piece,
            pl.BlockSpec(pos.shape, lambda i, s: (0, 0)),
        ],
        out_specs=[wide, pl.BlockSpec((2, window, head), lambda i, s: (0, 0, 0))],
        scratch_shapes=[
            pltpu.VMEM((window, head), low),
            pltpu.VMEM((head, window), low),
            pltpu.VMEM((window, head), low),
            pltpu.VMEM((window, head), f32),
            pltpu.VMEM((window, head), f32),
            pltpu.VMEM((pair, head, span), f32),
        ],
    )
    return pl.pallas_call(
        functools.partial(attend_back_kernel, scale, head**-0.5),
        grid_spec=spec,
        out_shape=(
            jax.ShapeDtypeStruct(query.shape, low),
            jax.ShapeDtypeStruct((2, window, head), low),
        ),
        compiler_params=pltpu.CompilerParams(vmem_limit_bytes=vmem_bytes),
        cost_estimate=pl.CostEstimate(
            flops=20 * work, bytes_accessed=8 * query.size, transcendentals=work // head
        ),
        name="attend_back",
    )(info, query, grad, attended, lse, near, far, pos)


def gelu_both(value, grad):
    inside = 0.7978845608028654 * (value + 0.044715 * value * value * value)
    bend = jnp.tanh(inside)
    half = 0.5 * (1.0 + bend)
    slope = half + 0.5 * value * (1.0 - bend * bend) * 0.7978845608028654 * (
        1.0 + 3.0 * 0.044715 * value * value
    )
    return (value * half).astype(low), (grad.astype(f32) * slope).astype(low)


def up_kernel(near_ref, far_ref, w_ref, b_ref, g_ref, act_ref, gh_ref, sum_ref, x_ref):
    rows = near_ref.shape[0]

    @pl.when(pl.program_id(0) == 0)
    def _():
        x_ref[:rows] = near_ref[...]
        x_ref[rows:] = far_ref[...]

    tile = min(256, w_ref.shape[1])
    for at in range(0, w_ref.shape[1], tile):
        cut = slice(at, at + tile)
        hidden = dot(x_ref[...], w_ref[:, cut]) + b_ref[:, cut]
        act, grad = gelu_both(hidden, g_ref[:, cut])
        act_ref[:, cut] = act
        gh_ref[:, cut] = grad
        sum_ref[:, cut] = jnp.sum(grad.astype(f32), axis=0, keepdims=True)


def up(near, far, w_up, bias, grad_act):
    rows, width = near.shape
    units = w_up.shape[1]
    tile = min(512, units)
    row = pl.BlockSpec((rows, width), lambda i: (0, 0))
    tall = pl.BlockSpec((2 * rows, tile), lambda i: (0, i))
    thin = pl.BlockSpec((1, tile), lambda i: (0, i))
    shape = jax.ShapeDtypeStruct((2 * rows, units), low)
    return pl.pallas_call(
        up_kernel,
        grid=(units // tile,),
        in_specs=[row, row, pl.BlockSpec((width, tile), lambda i: (0, i)), thin, tall],
        out_specs=[tall, tall, thin],
        out_shape=(shape, shape, jax.ShapeDtypeStruct((1, units), f32)),
        scratch_shapes=[pltpu.VMEM((2 * rows, width), low)],
        compiler_params=pltpu.CompilerParams(vmem_limit_bytes=vmem_bytes),
        cost_estimate=pl.CostEstimate(
            flops=4 * rows * width * units,
            bytes_accessed=2 * width * units + 16 * rows * units,
            transcendentals=2 * rows * units,
        ),
        name="up",
    )(near, far, w_up, bias.reshape(1, -1), grad_act)


def share_kernel(
    at, near_ref, far_ref, gnear_ref, gfar_ref, up_ref, down_ref, b_ref, act_ref, gh_ref, x_ref, g_ref
):
    rows = near_ref.shape[0]

    @pl.when(pl.program_id(0) == 0)
    def _():
        x_ref[:rows] = near_ref[...]
        x_ref[rows:] = far_ref[...]
        g_ref[:rows] = gnear_ref[...]
        g_ref[rows:] = gfar_ref[...]

    tile = min(256, up_ref.shape[1])
    for start in range(0, up_ref.shape[1], tile):
        cut = slice(start, start + tile)
        hidden = dot(x_ref[...], up_ref[:, cut]) + b_ref[:, cut]
        grad_act = contract_cols(g_ref[...], down_ref[cut, :])
        act, grad = gelu_both(hidden, grad_act)
        act_ref[:, cut] = act
        gh_ref[:, cut] = grad


def share(at, near, far, grad_near, grad_far, w_up, w_down, bias, units):
    rows, width = near.shape
    tile = min(512, units)
    tiles = units // tile
    row = pl.BlockSpec((rows, width), lambda i, s: (0, 0))
    tall = pl.BlockSpec((2 * rows, tile), lambda i, s: (0, i))
    shape = jax.ShapeDtypeStruct((2 * rows, units), low)
    spec = pltpu.PrefetchScalarGridSpec(
        num_scalar_prefetch=1,
        grid=(tiles,),
        in_specs=[
            row,
            row,
            row,
            row,
            pl.BlockSpec((width, tile), lambda i, s: (0, s[0] * tiles + i)),
            pl.BlockSpec((tile, width), lambda i, s: (s[0] * tiles + i, 0)),
            pl.BlockSpec((1, tile), lambda i, s: (0, s[0] * tiles + i)),
        ],
        out_specs=[tall, tall],
        scratch_shapes=[pltpu.VMEM((2 * rows, width), low)] * 2,
    )
    return pl.pallas_call(
        share_kernel,
        grid_spec=spec,
        out_shape=(shape, shape),
        compiler_params=pltpu.CompilerParams(vmem_limit_bytes=vmem_bytes),
        cost_estimate=pl.CostEstimate(
            flops=8 * rows * width * units,
            bytes_accessed=4 * width * units + 8 * rows * (units + width),
            transcendentals=2 * rows * units,
        ),
        name="share",
    )(at, near, far, grad_near, grad_far, w_up, w_down, bias.reshape(1, -1))


turns = ((3, 0), (1, 0), (3, 1), (2, 1), (1, 1), (2, 0), (0, 0), (0, 1))


def joined(items, place):
    if len(items) == 1:
        return items[0][...]
    start = 0
    for item in items:
        place[start : start + item.shape[0]] = item[...]
        start += item.shape[0]
    return place[...]


def store_turn(turn, result, outs):
    for index, out in enumerate(outs):

        @pl.when(turn // 2 == index)
        def _(out=out):
            out[0] = result.astype(out.dtype)


def hidden_kernel(lefts, at, *refs):
    left_refs, right_refs = refs[:lefts], refs[lefts:-6]
    outs, (left_place, right_place) = refs[-6:-2], refs[-2:]
    left = joined(left_refs, left_place)
    right = joined(right_refs, right_place)
    store_turn(pl.program_id(0), contract_rows(left, right), outs)


def hidden_weights(at, lefts, pieces, units, part, name):
    total = len(turns)
    span = lefts[0].shape[0]
    rows = span // 2
    half = units // 2
    depth = len(lefts) * span

    def left_of(own):
        def place(i, s):
            return (0, s[2 * total] * 2 + s[total + i] if own else s[total + i])

        return pl.BlockSpec((span, half), place)

    def out_of(index):
        return pl.BlockSpec((1, half, part), lambda i, s: (jnp.clip(i - 2 * index, 0, 1), 0, 0))

    spec = pltpu.PrefetchScalarGridSpec(
        num_scalar_prefetch=1,
        grid=(total,),
        in_specs=[left_of(n == 0) for n in range(len(lefts))]
        + [pl.BlockSpec((rows, part), lambda i, s: (0, s[i])) for _ in pieces],
        out_specs=[out_of(index) for index in range(4)],
        scratch_shapes=[pltpu.VMEM((depth, half), low), pltpu.VMEM((depth, part), low)],
    )
    return pl.pallas_call(
        functools.partial(hidden_kernel, len(lefts)),
        grid_spec=spec,
        out_shape=tuple(jax.ShapeDtypeStruct((2, half, part), low) for _ in range(4)),
        compiler_params=pltpu.CompilerParams(vmem_limit_bytes=60 * 1024 * 1024),
        cost_estimate=pl.CostEstimate(
            flops=2 * total * depth * half * part,
            bytes_accessed=4 * depth * (units + 4 * part),
            transcendentals=0,
        ),
        name=name,
    )(at, *lefts, *pieces)


def place_kernel(count, at, *refs):
    parts, (down_ref, up_ref) = refs[: 2 * count], refs[2 * count :]
    for step in range(count):

        @pl.when(pl.program_id(0) == step)
        def _(step=step):
            down_ref[...] = parts[step][0].astype(f32)
            up_ref[...] = parts[count + step][0].astype(f32).T


def place(at, downs, ups):
    count = len(downs)
    _, units, part = downs[0].shape
    piece = pl.BlockSpec((1, units, part), lambda i, s: (0, 0, 0))
    spec = pltpu.PrefetchScalarGridSpec(
        num_scalar_prefetch=1,
        grid=(count,),
        in_specs=[piece] * (2 * count),
        out_specs=[
            pl.BlockSpec((units, part), lambda i, s: (lax.rem(s[0] - i + count, count), 0)),
            pl.BlockSpec((part, units), lambda i, s: (0, lax.rem(s[0] - i + count, count))),
        ],
    )
    return pl.pallas_call(
        functools.partial(place_kernel, count),
        grid_spec=spec,
        out_shape=(
            jax.ShapeDtypeStruct((count * units, part), f32),
            jax.ShapeDtypeStruct((part, count * units), f32),
        ),
        compiler_params=pltpu.CompilerParams(vmem_limit_bytes=vmem_bytes),
        cost_estimate=pl.CostEstimate(
            flops=0, bytes_accessed=12 * count * units * part, transcendentals=0
        ),
        name="place",
    )(at, *downs, *ups)


def branch_kernel(at, near_ref, far_ref, y_ref, *refs):
    outs, place = refs[:4], refs[4]
    result = contract_rows(joined((near_ref, far_ref), place), y_ref[...])
    store_turn(pl.program_id(0), result, outs)


def branch_weights(at, near, far, right, part, name):
    total = len(turns)
    rows = near.shape[0]
    half = part // 2
    wide = right.shape[1]
    piece = pl.BlockSpec((rows, half), lambda i, s: (0, s[i] * 2 + s[total + i]))

    def all_of(item):
        return pl.BlockSpec(item.shape, lambda i, s: (0, 0))

    def out_of(index):
        return pl.BlockSpec((1, half, wide), lambda i, s: (jnp.clip(i - 2 * index, 0, 1), 0, 0))

    spec = pltpu.PrefetchScalarGridSpec(
        num_scalar_prefetch=1,
        grid=(total,),
        in_specs=[piece, piece, all_of(right)],
        out_specs=[out_of(index) for index in range(4)],
        scratch_shapes=[pltpu.VMEM((2 * rows, half), low)],
    )
    return pl.pallas_call(
        branch_kernel,
        grid_spec=spec,
        out_shape=tuple(jax.ShapeDtypeStruct((2, half, wide), low) for _ in range(4)),
        compiler_params=pltpu.CompilerParams(vmem_limit_bytes=vmem_bytes),
        cost_estimate=pl.CostEstimate(
            flops=4 * total * rows * half * wide,
            bytes_accessed=2 * total * half * wide,
            transcendentals=0,
        ),
        name=name,
    )(at, near, far, right)


def swap(item):
    return lax.ppermute(item, "tensor", [(0, 1), (1, 0)])


def cross(item, bits):
    size = lax.axis_size("dp")
    return lax.ppermute(item, "dp", [(i, i ^ bits) for i in range(size)])


def shift(item, by):
    size = lax.axis_size("seq")
    return lax.ppermute(item, "seq", [(i, (i + by) % size) for i in range(size)])


def shift_up(item, by):
    size = lax.axis_size("seq")
    return lax.ppermute(item, "seq", [(i, i + by) for i in range(size - by)])


def shift_down(item, by):
    size = lax.axis_size("seq")
    return lax.ppermute(item, "seq", [(i + by, i) for i in range(size - by)])


def pair_gather(item):
    return jnp.concatenate([item, swap(item)], axis=0)


def after(item, *others):
    return lax.optimization_barrier((item, *others))


def pair_sum(both):
    half = both.shape[0] // 2
    return both[:half].astype(f32) + swap(both[half:]).astype(f32)


def dp_first(parts, size):
    send_x, send_y, kept, own = (item.reshape(2, size, *item.shape[1:]) for item in parts)
    got_x = cross(send_x, 1)
    got_y = cross(send_y, 2)
    second_a = (kept[1].astype(f32) + got_x[0].astype(f32)).astype(low)
    second_b = (kept[0].astype(f32) + got_y[0].astype(f32)).astype(low)
    return second_a, second_b, own, got_x, got_y


def dp_second(second_a, second_b):
    return cross(second_a, 2), cross(second_b, 1)


def dp_join(own, got_x, got_y, last_a, last_b):
    return jnp.concatenate(
        [
            own[0].astype(f32) + got_x[1].astype(f32) + last_a.astype(f32),
            own[1].astype(f32) + got_y[1].astype(f32) + last_b.astype(f32),
        ],
        axis=1,
    )


def dp_last(second_a, second_b, own, got_x, got_y):
    return dp_join(own, got_x, got_y, *dp_second(second_a, second_b))


def norm_parts(rows):
    centre = rows - jnp.mean(rows, axis=-1, keepdims=True)
    inverse = lax.rsqrt(jnp.mean(centre * centre, axis=-1, keepdims=True) + epsilon)
    return centre * inverse, inverse


def norm_back(grad, unit, inverse, gain):
    scaled = grad * gain
    part = (
        scaled
        - jnp.mean(scaled, axis=-1, keepdims=True)
        - unit * jnp.mean(scaled * unit, axis=-1, keepdims=True)
    )
    return part * inverse, jnp.sum(grad * unit, axis=0), jnp.sum(grad, axis=0)


def on_device(
    tokens,
    lengths,
    ln1_gain,
    ln1_bias,
    w_query,
    b_query,
    w_key,
    w_value,
    b_value,
    w_out,
    b_out,
    ln2_gain,
    ln2_bias,
    w_up,
    b_up,
    w_down,
    b_down,
    cotangent,
):
    shard = tokens[0].astype(f32)
    rows_own, width = shard.shape
    seqs = lax.axis_size("seq")
    dps = lax.axis_size("dp")
    span = 2 * rows_own
    heads, head = b_query.shape
    at_dp, at_seq, at_core = (lax.axis_index(name) for name in ("dp", "seq", "tensor"))
    flip = at_core * rows_own
    span_start = at_seq * span
    hidden_local = w_up.shape[1]
    hidden_part = hidden_local // seqs
    dp_part = width // dps
    out_part = dp_part // seqs

    ends = jnp.cumsum(lengths[0], dtype=jnp.int32)
    row_pos = span_start + (jnp.arange(span, dtype=jnp.int32) ^ flip)
    row_start = jnp.max(
        jnp.where(row_pos[:, None] >= ends[None, :], ends[None, :], 0), axis=1
    ).astype(jnp.int32)
    pos = jnp.zeros((8, span), jnp.int32).at[0].set(row_pos).at[1].set(row_start)
    first, last = jnp.min(row_start), jnp.max(row_start)
    whole_to = jnp.clip(at_seq + 1 - (last + span - 1) // span, 1, at_seq + 1)
    some_to = jnp.clip(at_seq + 1 - first // span, whole_to, at_seq + 1)
    info = jnp.stack([whole_to, some_to, at_seq, flip]).astype(jnp.int32)

    unit_one, inverse_one = norm_parts(shard)
    normed = (unit_one * ln1_gain + ln1_bias).astype(low)
    w_both = jnp.concatenate([w_key, w_value], axis=1)
    b_both = jnp.concatenate([jnp.zeros_like(b_value), b_value])
    both_own = (dot(normed, w_both) + b_both).astype(low)
    pieces = [shift_up(both_own, by) for by in range(1, seqs)]
    grad_own = cotangent[0]
    grad_own, both_own = after(grad_own, both_own)
    grad_held = [grad_own]
    for step in range(1, seqs):
        grad_held.append(shift(grad_held[-1], 1))
    grad_far = [swap(grad_own)]
    grad_act = contract_cols(jnp.concatenate([grad_own, grad_far[0]], axis=0), w_down).astype(low)
    grad_act, *pieces = after(grad_act, *pieces)
    near = jnp.stack([both_own] + pieces)
    far = swap(near)
    normed_far = swap(normed)
    normed_all = jnp.concatenate([normed, normed_far], axis=0)
    query = (dot(normed_all, w_query) + b_query.reshape(-1)).astype(low)

    if seqs > 1:
        query, grad_held[1] = after(query, grad_held[1])
    attended, lse = attend(info, query, near, far, pos, heads, head)
    if seqs > 2:
        attended, grad_held[2] = after(attended, grad_held[2])
    middle = shard + (pair_sum(dot(attended, w_out).astype(low)) + b_out)
    unit_two, inverse_two = norm_parts(middle)
    normed_two = (unit_two * ln2_gain + ln2_bias).astype(low)

    held = [normed_two]
    for step in range(1, seqs):
        held.append(shift(held[-1], 1))
    held_far = [swap(normed_two)]
    activated, grad_hidden, grad_b_up = up(held[0], held_far[0], w_up, b_up, grad_act)
    if seqs > 3:
        grad_hidden, grad_held[3] = after(grad_hidden, grad_held[3])
    grad_normed_two = contract_cols(grad_hidden, w_up).astype(low)
    grad_normed_two = pair_sum(grad_normed_two)
    result = dot(activated, w_down).astype(low)
    grad_normed_two, result, *held[1:2] = after(grad_normed_two, result, *held[1:2])

    back, grad_ln2_gain, grad_ln2_bias = norm_back(
        grad_normed_two, unit_two, inverse_two, ln2_gain
    )
    grad_out = grad_own.astype(f32)
    grad_b_down = jnp.sum(grad_out, axis=0)
    grad_middle = grad_out + back
    grad_branch = grad_middle.astype(low)
    grad_b_out = jnp.sum(grad_branch.astype(f32), axis=0)
    grad_branch_far = swap(grad_branch)
    grad_branch_all = jnp.concatenate([grad_branch, grad_branch_far], axis=0)
    grad_attended = contract_cols(grad_branch_all, w_out).astype(low)
    blocks = [at_dp ^ r for r, _ in turns]
    halves = [jnp.int32(half) for _, half in turns]
    table = jnp.stack(blocks + halves + [at_seq, at_core]).astype(jnp.int32)

    parts_out = branch_weights(
        table, grad_branch, grad_branch_far, attended, dp_part, "weight_out"
    )

    share_at = at_seq.reshape(1).astype(jnp.int32)
    acts, grads = [activated], [grad_hidden]

    def shared_part(step):
        held_far.append(swap(held[step]))
        grad_far.append(swap(grad_held[step]))
        act, grad = share(
            share_at,
            held[step],
            held_far[step],
            grad_held[step],
            grad_far[step],
            w_up,
            w_down,
            b_up,
            hidden_part,
        )
        acts.append(act)
        grads.append(grad)

    if seqs > 2:
        shared_part(1)
        grad_attended, acts[1], held[2], *parts_out = after(
            grad_attended, acts[1], held[2], *parts_out
        )
        for step in range(3, seqs):
            held[step] = shift(held[step - 1], 1)
    first_out = dp_first(parts_out, 1)

    def to_seq(item, by, axis):
        at = lax.rem(at_seq + by, seqs)
        return lax.dynamic_slice_in_dim(item, at * out_part, out_part, axis)

    grad_query, grad_both = attend_back(
        info, query, grad_attended, attended, lse, near, far, pos, heads, head
    )
    seconds = first_out[:2]
    if seqs > 1:
        grad_query, grad_both, held[-1], *seconds = after(
            grad_query, grad_both, held[-1], *seconds
        )
    last_out = dp_second(*seconds)

    for step in range(len(acts), seqs):
        shared_part(step)
    acts[-1], *last_out = after(acts[-1], *last_out)
    sum_out = dp_join(*first_out[2:], *last_out)[0]
    downs = hidden_weights(
        table,
        acts,
        [item for couple in zip(grad_held, grad_far) for item in couple],
        hidden_part,
        dp_part,
        "weight_down",
    )
    grads[0], sum_out, *downs = after(grads[0], sum_out, *downs)
    first_down = dp_first(downs, 1)
    narrow = sum_out.astype(low)
    out_parts = [shift(to_seq(narrow, by, 0), by) for by in range(1, seqs)]
    ups = hidden_weights(
        table,
        grads,
        [item for couple in zip(held, held_far) for item in couple],
        hidden_part,
        dp_part,
        "weight_up",
    )
    grad_query, grad_both, *rest = after(grad_query, grad_both, *first_down[:2], *ups, *out_parts)
    last_down = dp_second(*rest[:2])
    first_up = dp_first(rest[2:6], 1)
    out_parts = rest[6:]

    grad_both = grad_both.reshape(2, seqs, 2, rows_own, head)
    kept = lax.dynamic_index_in_dim(grad_both, at_core, 0, False)
    given = lax.dynamic_index_in_dim(grad_both, 1 - at_core, 0, False)
    grad_kv = (kept.astype(f32) + swap(given)[:, ::-1].astype(f32)).astype(low)
    grad_kv = grad_kv.reshape(seqs, span, head)
    total = grad_kv[0].astype(f32)
    for by in range(1, seqs):
        total = total + shift_down(grad_kv[by], by).astype(f32)
    grad_kv = total.astype(low)
    grad_qkv = jnp.concatenate([grad_query, grad_kv], axis=1)
    w_qkv = jnp.concatenate([w_query, jnp.where(at_core == 0, w_key, w_value)], axis=1)
    grad_normed = contract_cols(grad_qkv, w_qkv).astype(low)
    grad_normed, *last_down = after(grad_normed, *last_down)
    grad_normed = pair_sum(grad_normed)
    sum_down = dp_join(*first_down[2:], *last_down).astype(low)

    downs = [to_seq(sum_down, by, 2) for by in range(seqs)]
    grad_qkv, *downs = after(grad_qkv, *downs)
    downs = [downs[0]] + [shift(downs[by], by) for by in range(1, seqs)]
    parts = branch_weights(table, normed, normed_far, grad_qkv, dp_part, "weight_query")
    rest = after(*parts, *first_up[:2])
    first_query = dp_first(rest[:4], 1)
    last_up = dp_second(*rest[4:6])

    back, grad_ln1_gain, grad_ln1_bias = norm_back(
        grad_normed, unit_one, inverse_one, ln1_gain
    )
    grad_input = (grad_middle + back).astype(low)[None]
    grad_b_value = jnp.where(at_core == 1, jnp.sum(grad_kv.astype(f32), axis=0), 0.0)
    grad_b_query = jnp.sum(grad_query.astype(f32), axis=0)
    features = [
        grad_ln1_gain,
        grad_ln1_bias,
        grad_b_out,
        grad_ln2_gain,
        grad_ln2_bias,
        grad_b_down,
    ]
    count = len(features)
    features = jnp.concatenate([item.reshape(-1, head) for item in features], axis=0)
    rows = features.shape[0]
    features = features + swap(features)
    values = grad_b_value.reshape(1, head)
    values = values + swap(values)
    packed = jnp.concatenate(
        [
            features,
            grad_b_up.reshape(-1, head),
            grad_b_query.reshape(-1, head),
            jnp.broadcast_to(values, (8, head)),
        ],
        axis=0,
    )
    rest = after(packed, *last_up, *first_query[:2], *downs)
    packed, last_up, downs = rest[0], rest[1:3], rest[5:]
    last_query = dp_second(*rest[3:5])
    sum_up = dp_join(*first_up[2:], *last_up).astype(low)
    ups = [to_seq(sum_up, 0, 2)]
    for by in range(1, seqs):
        ups.append(shift(to_seq(sum_up, by, 2), by))
    total = packed + cross(packed, 1) + cross(packed, 2) + cross(packed, 3)
    total, *last_query = after(total, *last_query)
    packed = total
    for by in range(1, seqs):
        total = total + shift(packed, by)
    sum_query = dp_join(*first_query[2:], *last_query)[0]
    narrow = sum_query.astype(low)
    query_parts = [to_seq(narrow, by, 0) for by in range(1, seqs)]
    share_at, *query_parts = after(share_at, *query_parts)
    query_parts = [shift(item, by + 1) for by, item in enumerate(query_parts)]
    output = (middle + (pair_sum(result) + b_down)).astype(low)[None]
    out_w_down, out_w_up = place(share_at, downs, ups)

    out_qkv = to_seq(sum_query, 0, 0)
    for item in query_parts:
        out_qkv = out_qkv + item.astype(f32)
    out_w_out = to_seq(sum_out, 0, 0)
    for item in out_parts:
        out_w_out = out_w_out + item.astype(f32)
    out_w_out = out_w_out.T
    out_w_query = out_qkv[:, : heads * head]
    half = out_part // 2
    last_kv = out_qkv[:, heads * head :]
    mine = lax.dynamic_slice_in_dim(last_kv, at_core * half, half, 0)
    other = swap(lax.dynamic_slice_in_dim(last_kv, (1 - at_core) * half, half, 0))
    out_w_key = jnp.where(at_core == 0, mine, other)
    out_w_value = jnp.where(at_core == 0, other, mine)

    place_own = at_dp * seqs + at_seq

    def own_part(item, size, index):
        return lax.dynamic_slice_in_dim(item, index * size, size, item.ndim - 1)

    vectors = own_part(
        total[:rows].reshape(count, width), out_part // 2, place_own * 2 + at_core
    )
    thin = head // (dps * seqs)
    up_rows = b_up.shape[0]
    sum_b_up = own_part(total[rows : rows + up_rows], thin, place_own)
    sum_b_query = own_part(total[rows + up_rows : rows + up_rows + heads], thin, place_own)
    sum_b_value = own_part(total[rows + up_rows + heads], thin // 2, place_own * 2 + at_core)
    return (
        output,
        grad_input,
        vectors[0],
        vectors[1],
        out_w_query,
        sum_b_query,
        out_w_key,
        out_w_value,
        sum_b_value,
        out_w_out,
        vectors[2],
        vectors[3],
        vectors[4],
        out_w_up,
        sum_b_up,
        out_w_down,
        vectors[5],
    )


def solution(mesh):
    in_specs = (
        P("dp", ("seq", "tensor"), None),
        P("dp", None),
        P(),
        P(),
        P(None, "tensor"),
        P("tensor", None),
        P(),
        P(),
        P(),
        P("tensor", None),
        P(),
        P(),
        P(),
        P(None, "tensor"),
        P("tensor", None),
        P("tensor", None),
        P(),
        P("dp", ("seq", "tensor"), None),
    )
    out_specs = (
        P("dp", ("seq", "tensor"), None),
        P("dp", ("seq", "tensor"), None),
        P(("dp", "seq", "tensor")),
        P(("dp", "seq", "tensor")),
        P(("dp", "seq"), "tensor"),
        P("tensor", ("dp", "seq")),
        P(("dp", "seq", "tensor"), None),
        P(("dp", "seq", "tensor"), None),
        P(("dp", "seq", "tensor")),
        P("tensor", ("dp", "seq")),
        P(("dp", "seq", "tensor")),
        P(("dp", "seq", "tensor")),
        P(("dp", "seq", "tensor")),
        P(("dp", "seq"), "tensor"),
        P("tensor", ("dp", "seq")),
        P("tensor", ("dp", "seq")),
        P(("dp", "seq", "tensor")),
    )
    return jax.shard_map(
        on_device, mesh=mesh, in_specs=in_specs, out_specs=out_specs, check_vma=False
    )
```

```python
import functools

import jax
import jax.numpy as jnp
from jax import lax
from jax.experimental import pallas as pl
from jax.experimental.pallas import tpu as pltpu
from jax.sharding import PartitionSpec as P

epsilon = 1e-05
negative = -1e30
log2e = 1.4426950408889634
f32 = jnp.float32
low = jnp.bfloat16
vmem_bytes = 48 * 1024 * 1024


def dot(left, right):
    return jnp.dot(left, right, preferred_element_type=f32)


def contract_rows(left, right):
    return lax.dot_general(left, right, (((0,), (0,)), ((), ())), preferred_element_type=f32)


def contract_cols(left, right):
    return lax.dot_general(left, right, (((1,), (1,)), ((), ())), preferred_element_type=f32)


def allowed_mask(start, base, flip, pos_ref):
    offset = lax.broadcasted_iota(jnp.int32, (start, 1), 0)
    key_pos = base + (offset ^ flip)
    return (key_pos <= pos_ref[0:1, :]) & (key_pos >= pos_ref[1:2, :])


def over_blocks(info, body):
    body(0, True)
    lax.fori_loop(1, info[0], lambda s, c: (body(s, False), c)[1], 0)
    lax.fori_loop(info[0], info[1], lambda s, c: (body(s, True), c)[1], 0)


def gather_keys(near_ref, far_ref, head, places):
    rows = near_ref.shape[1]

    def one(s, carry):
        for side, ref in enumerate((near_ref, far_ref)):
            where = pl.multiple_of(s * 2 * rows + side * rows, rows)
            item = ref[s]
            for kind, target in enumerate(places):
                for turned, place in target:
                    part = item[:, kind * head : (kind + 1) * head]
                    if turned:
                        place[:, pl.ds(where, rows)] = part.T
                    else:
                        place[pl.ds(where, rows), :] = part
        return carry

    lax.fori_loop(0, near_ref.shape[0], one, 0)


def attend_kernel(
    scale,
    info,
    q_ref,
    near_ref,
    far_ref,
    pos_ref,
    o_ref,
    lse_ref,
    k_ref,
    vt_ref,
    m_ref,
    l_ref,
    acc_ref,
):
    span = q_ref.shape[0]
    head = k_ref.shape[1]
    pair = q_ref.shape[1] // head
    step = pl.program_id(0)

    @pl.when(step == 0)
    def _():
        gather_keys(near_ref, far_ref, head, [[(False, k_ref)], [(True, vt_ref)]])

    turned = [q_ref[:, h * head : (h + 1) * head].T for h in range(pair)]
    m_ref[...] = jnp.full_like(m_ref, negative)
    l_ref[...] = jnp.zeros_like(l_ref)
    acc_ref[...] = jnp.zeros_like(acc_ref)

    def body(s, masked):
        where = pl.multiple_of(s * span, span)
        key_block = k_ref[pl.ds(where, span), :]
        value_block = vt_ref[:, pl.ds(where, span)]
        if masked:
            allowed = allowed_mask(span, (info[2] - s) * span, info[3], pos_ref)
        for h in range(pair):
            scores = dot(key_block, turned[h]) * scale
            if masked:
                scores = jnp.where(allowed, scores, negative)
            before = m_ref[h]
            after = jnp.maximum(before, jnp.max(scores, axis=0, keepdims=True))
            weights = jnp.exp2(scores - after)
            shrink = jnp.exp2(before - after)
            m_ref[h] = after
            l_ref[h] = l_ref[h] * shrink + jnp.sum(weights, axis=0, keepdims=True)
            acc_ref[h] = acc_ref[h] * shrink + dot(value_block, weights.astype(low))

    over_blocks(info, body)
    for h in range(pair):
        total = l_ref[h]
        lse_ref[pl.ds(step * pair + h, 1), :] = m_ref[h] + jnp.log2(total)
        o_ref[:, h * head : (h + 1) * head] = (acc_ref[h] / total).T.astype(low)


def attend_back_kernel(
    scale,
    unit,
    info,
    q_ref,
    do_ref,
    o_ref,
    lse_ref,
    near_ref,
    far_ref,
    pos_ref,
    dq_ref,
    dkv_ref,
    k_ref,
    kt_ref,
    v_ref,
    dk_ref,
    dv_ref,
    dqt_ref,
):
    span = q_ref.shape[0]
    head = k_ref.shape[1]
    pair = q_ref.shape[1] // head
    step = pl.program_id(0)

    @pl.when(step == 0)
    def _():
        dk_ref[...] = jnp.zeros_like(dk_ref)
        dv_ref[...] = jnp.zeros_like(dv_ref)
        gather_keys(
            near_ref, far_ref, head, [[(False, k_ref), (True, kt_ref)], [(False, v_ref)]]
        )

    dqt_ref[...] = jnp.zeros_like(dqt_ref)
    queries = [q_ref[:, h * head : (h + 1) * head] for h in range(pair)]
    grads = [do_ref[:, h * head : (h + 1) * head] for h in range(pair)]
    queries_t = [item.T for item in queries]
    grads_t = [item.T for item in grads]
    inner = [
        jnp.sum(
            grads_t[h].astype(f32) * o_ref[:, h * head : (h + 1) * head].T.astype(f32),
            axis=0,
            keepdims=True,
        )
        for h in range(pair)
    ]
    totals = [lse_ref[pl.ds(step * pair + h, 1), :] for h in range(pair)]

    def body(s, masked):
        where = pl.multiple_of(s * span, span)
        key_block = k_ref[pl.ds(where, span), :]
        key_turned = kt_ref[:, pl.ds(where, span)]
        value_block = v_ref[pl.ds(where, span), :]
        if masked:
            allowed = allowed_mask(span, (info[2] - s) * span, info[3], pos_ref)
        key_part = jnp.zeros((span, head), f32)
        value_part = jnp.zeros((span, head), f32)
        for h in range(pair):
            scores = dot(key_block, queries_t[h]) * scale - totals[h]
            if masked:
                scores = jnp.where(allowed, scores, negative)
            probs = jnp.exp2(scores)
            grad_probs = dot(value_block, grads_t[h])
            grad_scores = (probs * (grad_probs - inner[h])).astype(low)
            key_part += dot(grad_scores, queries[h])
            value_part += dot(probs.astype(low), grads[h])
            dqt_ref[h] += dot(key_turned, grad_scores)
        dk_ref[pl.ds(where, span), :] += key_part
        dv_ref[pl.ds(where, span), :] += value_part

    over_blocks(info, body)
    for h in range(pair):
        dq_ref[:, h * head : (h + 1) * head] = (dqt_ref[h] * unit).T.astype(low)

    @pl.when(step == pl.num_programs(0) - 1)
    def _():
        dkv_ref[0] = (dk_ref[...] * unit).astype(low)
        dkv_ref[1] = dv_ref[...].astype(low)


def attend(info, query, near, far, pos, heads, head):
    span = query.shape[0]
    window = near.shape[0] * span
    pair = 2
    scale = head**-0.5 * log2e
    work = heads * span * window * head
    piece = pl.BlockSpec(near.shape, lambda i, s: (0, 0, 0))
    spec = pltpu.PrefetchScalarGridSpec(
        num_scalar_prefetch=1,
        grid=(heads // pair,),
        in_specs=[
            pl.BlockSpec((span, pair * head), lambda i, s: (0, i)),
            piece,
            piece,
            pl.BlockSpec(pos.shape, lambda i, s: (0, 0)),
        ],
        out_specs=[
            pl.BlockSpec((span, pair * head), lambda i, s: (0, i)),
            pl.BlockSpec((heads, span), lambda i, s: (0, 0)),
        ],
        scratch_shapes=[
            pltpu.VMEM((window, head), low),
            pltpu.VMEM((head, window), low),
            pltpu.VMEM((pair, 1, span), f32),
            pltpu.VMEM((pair, 1, span), f32),
            pltpu.VMEM((pair, head, span), f32),
        ],
    )
    return pl.pallas_call(
        functools.partial(attend_kernel, scale),
        grid_spec=spec,
        out_shape=(
            jax.ShapeDtypeStruct(query.shape, low),
            jax.ShapeDtypeStruct((heads, span), f32),
        ),
        compiler_params=pltpu.CompilerParams(vmem_limit_bytes=vmem_bytes),
        cost_estimate=pl.CostEstimate(
            flops=8 * work, bytes_accessed=4 * query.size, transcendentals=work // head
        ),
        name="attend",
    )(info, query, near, far, pos)


def attend_back(info, query, grad, attended, lse, near, far, pos, heads, head):
    span = query.shape[0]
    window = near.shape[0] * span
    pair = 2
    scale = head**-0.5 * log2e
    work = heads * span * window * head
    wide = pl.BlockSpec((span, pair * head), lambda i, s: (0, i))
    piece = pl.BlockSpec(near.shape, lambda i, s: (0, 0, 0))
    spec = pltpu.PrefetchScalarGridSpec(
        num_scalar_prefetch=1,
        grid=(heads // pair,),
        in_specs=[
            wide,
            wide,
            wide,
            pl.BlockSpec((heads, span), lambda i, s: (0, 0)),
            piece,
            piece,
            pl.BlockSpec(pos.shape, lambda i, s: (0, 0)),
        ],
        out_specs=[wide, pl.BlockSpec((2, window, head), lambda i, s: (0, 0, 0))],
        scratch_shapes=[
            pltpu.VMEM((window, head), low),
            pltpu.VMEM((head, window), low),
            pltpu.VMEM((window, head), low),
            pltpu.VMEM((window, head), f32),
            pltpu.VMEM((window, head), f32),
            pltpu.VMEM((pair, head, span), f32),
        ],
    )
    return pl.pallas_call(
        functools.partial(attend_back_kernel, scale, head**-0.5),
        grid_spec=spec,
        out_shape=(
            jax.ShapeDtypeStruct(query.shape, low),
            jax.ShapeDtypeStruct((2, window, head), low),
        ),
        compiler_params=pltpu.CompilerParams(vmem_limit_bytes=vmem_bytes),
        cost_estimate=pl.CostEstimate(
            flops=20 * work, bytes_accessed=8 * query.size, transcendentals=work // head
        ),
        name="attend_back",
    )(info, query, grad, attended, lse, near, far, pos)


def gelu_both(value, grad):
    inside = 0.7978845608028654 * (value + 0.044715 * value * value * value)
    bend = jnp.tanh(inside)
    half = 0.5 * (1.0 + bend)
    slope = half + 0.5 * value * (1.0 - bend * bend) * 0.7978845608028654 * (
        1.0 + 3.0 * 0.044715 * value * value
    )
    return (value * half).astype(low), (grad.astype(f32) * slope).astype(low)


def up_kernel(near_ref, far_ref, w_ref, b_ref, g_ref, act_ref, gh_ref, sum_ref, x_ref):
    rows = near_ref.shape[0]

    @pl.when(pl.program_id(0) == 0)
    def _():
        x_ref[:rows] = near_ref[...]
        x_ref[rows:] = far_ref[...]

    tile = min(256, w_ref.shape[1])
    for at in range(0, w_ref.shape[1], tile):
        cut = slice(at, at + tile)
        hidden = dot(x_ref[...], w_ref[:, cut]) + b_ref[:, cut]
        act, grad = gelu_both(hidden, g_ref[:, cut])
        act_ref[:, cut] = act
        gh_ref[:, cut] = grad
        sum_ref[:, cut] = jnp.sum(grad.astype(f32), axis=0, keepdims=True)


def up(near, far, w_up, bias, grad_act):
    rows, width = near.shape
    units = w_up.shape[1]
    tile = min(512, units)
    row = pl.BlockSpec((rows, width), lambda i: (0, 0))
    tall = pl.BlockSpec((2 * rows, tile), lambda i: (0, i))
    thin = pl.BlockSpec((1, tile), lambda i: (0, i))
    shape = jax.ShapeDtypeStruct((2 * rows, units), low)
    return pl.pallas_call(
        up_kernel,
        grid=(units // tile,),
        in_specs=[row, row, pl.BlockSpec((width, tile), lambda i: (0, i)), thin, tall],
        out_specs=[tall, tall, thin],
        out_shape=(shape, shape, jax.ShapeDtypeStruct((1, units), f32)),
        scratch_shapes=[pltpu.VMEM((2 * rows, width), low)],
        compiler_params=pltpu.CompilerParams(vmem_limit_bytes=vmem_bytes),
        cost_estimate=pl.CostEstimate(
            flops=4 * rows * width * units,
            bytes_accessed=2 * width * units + 16 * rows * units,
            transcendentals=2 * rows * units,
        ),
        name="up",
    )(near, far, w_up, bias.reshape(1, -1), grad_act)


def share_kernel(
    at, near_ref, far_ref, gnear_ref, gfar_ref, up_ref, down_ref, b_ref, act_ref, gh_ref, x_ref, g_ref
):
    rows = near_ref.shape[0]

    @pl.when(pl.program_id(0) == 0)
    def _():
        x_ref[:rows] = near_ref[...]
        x_ref[rows:] = far_ref[...]
        g_ref[:rows] = gnear_ref[...]
        g_ref[rows:] = gfar_ref[...]

    tile = min(256, up_ref.shape[1])
    for start in range(0, up_ref.shape[1], tile):
        cut = slice(start, start + tile)
        hidden = dot(x_ref[...], up_ref[:, cut]) + b_ref[:, cut]
        grad_act = contract_cols(g_ref[...], down_ref[cut, :])
        act, grad = gelu_both(hidden, grad_act)
        act_ref[:, cut] = act
        gh_ref[:, cut] = grad


def share(at, near, far, grad_near, grad_far, w_up, w_down, bias, units):
    rows, width = near.shape
    tile = min(512, units)
    tiles = units // tile
    row = pl.BlockSpec((rows, width), lambda i, s: (0, 0))
    tall = pl.BlockSpec((2 * rows, tile), lambda i, s: (0, i))
    shape = jax.ShapeDtypeStruct((2 * rows, units), low)
    spec = pltpu.PrefetchScalarGridSpec(
        num_scalar_prefetch=1,
        grid=(tiles,),
        in_specs=[
            row,
            row,
            row,
            row,
            pl.BlockSpec((width, tile), lambda i, s: (0, s[0] * tiles + i)),
            pl.BlockSpec((tile, width), lambda i, s: (s[0] * tiles + i, 0)),
            pl.BlockSpec((1, tile), lambda i, s: (0, s[0] * tiles + i)),
        ],
        out_specs=[tall, tall],
        scratch_shapes=[pltpu.VMEM((2 * rows, width), low)] * 2,
    )
    return pl.pallas_call(
        share_kernel,
        grid_spec=spec,
        out_shape=(shape, shape),
        compiler_params=pltpu.CompilerParams(vmem_limit_bytes=vmem_bytes),
        cost_estimate=pl.CostEstimate(
            flops=8 * rows * width * units,
            bytes_accessed=4 * width * units + 8 * rows * (units + width),
            transcendentals=2 * rows * units,
        ),
        name="share",
    )(at, near, far, grad_near, grad_far, w_up, w_down, bias.reshape(1, -1))


turns = ((3, 0), (1, 0), (3, 1), (2, 1), (1, 1), (2, 0), (0, 0), (0, 1))


def joined(items, place):
    if len(items) == 1:
        return items[0][...]
    start = 0
    for item in items:
        place[start : start + item.shape[0]] = item[...]
        start += item.shape[0]
    return place[...]


def store_turn(turn, result, outs):
    for index, out in enumerate(outs):

        @pl.when(turn // 2 == index)
        def _(out=out):
            out[0] = result.astype(out.dtype)


def hidden_kernel(lefts, at, *refs):
    left_refs, right_refs = refs[:lefts], refs[lefts:-6]
    (send_x, send_y, kept, own), (left_place, right_place) = refs[-6:-2], refs[-2:]
    step = pl.program_id(0)

    @pl.when(step == 0)
    def _():
        start = 0
        for item in left_refs:
            left_place[start : start + item.shape[0]] = item[...]
            start += item.shape[0]

    result = contract_rows(left_place[...], joined(right_refs, right_place)).astype(low)
    half = result.shape[0] // 2
    first, second = result[:half], result[half:]

    @pl.when(step == 0)
    def _():
        send_x[0] = first
        send_y[0] = second

    @pl.when(step == 1)
    def _():
        send_x[0] = first
        kept[0] = second

    @pl.when(step == 2)
    def _():
        kept[0] = first
        send_y[0] = second

    @pl.when(step == 3)
    def _():
        own[0] = first
        own[1] = second


def hidden_weights(at, lefts, pieces, units, part, name):
    span = lefts[0].shape[0]
    rows = span // 2
    half = units // 2
    depth = len(lefts) * span

    def left_of(own):
        return pl.BlockSpec((span, units), lambda i, s: (0, s[4] if own else 0))

    thin = (1, half, part)
    spec = pltpu.PrefetchScalarGridSpec(
        num_scalar_prefetch=1,
        grid=(4,),
        in_specs=[left_of(n == 0) for n in range(len(lefts))]
        + [pl.BlockSpec((rows, part), lambda i, s: (0, s[i])) for _ in pieces],
        out_specs=[
            pl.BlockSpec(thin, lambda i, s: (jnp.clip(i, 0, 1), 0, 0)),
            pl.BlockSpec(thin, lambda i, s: (i // 2, 0, 0)),
            pl.BlockSpec(thin, lambda i, s: (i // 2, 0, 0)),
            pl.BlockSpec((2, half, part), lambda i, s: (0, 0, 0)),
        ],
        scratch_shapes=[pltpu.VMEM((depth, units), low), pltpu.VMEM((depth, part), low)],
    )
    return pl.pallas_call(
        functools.partial(hidden_kernel, len(lefts)),
        grid_spec=spec,
        out_shape=tuple(jax.ShapeDtypeStruct((2, half, part), low) for _ in range(4)),
        compiler_params=pltpu.CompilerParams(vmem_limit_bytes=60 * 1024 * 1024),
        cost_estimate=pl.CostEstimate(
            flops=8 * depth * units * part,
            bytes_accessed=4 * depth * (units + 4 * part),
            transcendentals=0,
        ),
        name=name,
    )(at, *lefts, *pieces)


def place_kernel(count, at, *refs):
    parts, (down_ref, up_ref) = refs[: 2 * count], refs[2 * count :]
    for step in range(count):

        @pl.when(pl.program_id(0) == step)
        def _(step=step):
            down_ref[...] = parts[step][0].astype(f32)
            up_ref[...] = parts[count + step][0].astype(f32).T


def place(at, downs, ups):
    count = len(downs)
    _, units, part = downs[0].shape
    piece = pl.BlockSpec((1, units, part), lambda i, s: (0, 0, 0))
    spec = pltpu.PrefetchScalarGridSpec(
        num_scalar_prefetch=1,
        grid=(count,),
        in_specs=[piece] * (2 * count),
        out_specs=[
            pl.BlockSpec((units, part), lambda i, s: (lax.rem(s[0] - i + count, count), 0)),
            pl.BlockSpec((part, units), lambda i, s: (0, lax.rem(s[0] - i + count, count))),
        ],
    )
    return pl.pallas_call(
        functools.partial(place_kernel, count),
        grid_spec=spec,
        out_shape=(
            jax.ShapeDtypeStruct((count * units, part), f32),
            jax.ShapeDtypeStruct((part, count * units), f32),
        ),
        compiler_params=pltpu.CompilerParams(vmem_limit_bytes=vmem_bytes),
        cost_estimate=pl.CostEstimate(
            flops=0, bytes_accessed=12 * count * units * part, transcendentals=0
        ),
        name="place",
    )(at, *downs, *ups)


def branch_kernel(at, near_ref, far_ref, y_ref, *refs):
    outs, place = refs[:4], refs[4]
    result = contract_rows(joined((near_ref, far_ref), place), y_ref[...])
    store_turn(pl.program_id(0), result, outs)


def branch_weights(at, near, far, right, part, name):
    total = len(turns)
    rows = near.shape[0]
    half = part // 2
    wide = right.shape[1]
    piece = pl.BlockSpec((rows, half), lambda i, s: (0, s[i] * 2 + s[total + i]))

    def all_of(item):
        return pl.BlockSpec(item.shape, lambda i, s: (0, 0))

    def out_of(index):
        return pl.BlockSpec((1, half, wide), lambda i, s: (jnp.clip(i - 2 * index, 0, 1), 0, 0))

    spec = pltpu.PrefetchScalarGridSpec(
        num_scalar_prefetch=1,
        grid=(total,),
        in_specs=[piece, piece, all_of(right)],
        out_specs=[out_of(index) for index in range(4)],
        scratch_shapes=[pltpu.VMEM((2 * rows, half), low)],
    )
    return pl.pallas_call(
        branch_kernel,
        grid_spec=spec,
        out_shape=tuple(jax.ShapeDtypeStruct((2, half, wide), low) for _ in range(4)),
        compiler_params=pltpu.CompilerParams(vmem_limit_bytes=vmem_bytes),
        cost_estimate=pl.CostEstimate(
            flops=4 * total * rows * half * wide,
            bytes_accessed=2 * total * half * wide,
            transcendentals=0,
        ),
        name=name,
    )(at, near, far, right)


def swap(item):
    return lax.ppermute(item, "tensor", [(0, 1), (1, 0)])


def cross(item, bits):
    size = lax.axis_size("dp")
    return lax.ppermute(item, "dp", [(i, i ^ bits) for i in range(size)])


def shift(item, by):
    size = lax.axis_size("seq")
    return lax.ppermute(item, "seq", [(i, (i + by) % size) for i in range(size)])


def shift_up(item, by):
    size = lax.axis_size("seq")
    return lax.ppermute(item, "seq", [(i, i + by) for i in range(size - by)])


def shift_down(item, by):
    size = lax.axis_size("seq")
    return lax.ppermute(item, "seq", [(i + by, i) for i in range(size - by)])


def pair_gather(item):
    return jnp.concatenate([item, swap(item)], axis=0)


def after(item, *others):
    return lax.optimization_barrier((item, *others))


def pair_sum(both):
    half = both.shape[0] // 2
    return both[:half].astype(f32) + swap(both[half:]).astype(f32)


def dp_first(parts, size):
    send_x, send_y, kept, own = (item.reshape(2, size, *item.shape[1:]) for item in parts)
    got_x = cross(send_x, 1)
    got_y = cross(send_y, 2)
    second_a = (kept[1].astype(f32) + got_x[0].astype(f32)).astype(low)
    second_b = (kept[0].astype(f32) + got_y[0].astype(f32)).astype(low)
    return second_a, second_b, own, got_x, got_y


def dp_second(second_a, second_b):
    return cross(second_a, 2), cross(second_b, 1)


def dp_join(own, got_x, got_y, last_a, last_b):
    return jnp.concatenate(
        [
            own[0].astype(f32) + got_x[1].astype(f32) + last_a.astype(f32),
            own[1].astype(f32) + got_y[1].astype(f32) + last_b.astype(f32),
        ],
        axis=1,
    )


def dp_last(second_a, second_b, own, got_x, got_y):
    return dp_join(own, got_x, got_y, *dp_second(second_a, second_b))


def norm_parts(rows):
    centre = rows - jnp.mean(rows, axis=-1, keepdims=True)
    inverse = lax.rsqrt(jnp.mean(centre * centre, axis=-1, keepdims=True) + epsilon)
    return centre * inverse, inverse


def norm_back(grad, unit, inverse, gain):
    scaled = grad * gain
    part = (
        scaled
        - jnp.mean(scaled, axis=-1, keepdims=True)
        - unit * jnp.mean(scaled * unit, axis=-1, keepdims=True)
    )
    return part * inverse, jnp.sum(grad * unit, axis=0), jnp.sum(grad, axis=0)


def on_device(
    tokens,
    lengths,
    ln1_gain,
    ln1_bias,
    w_query,
    b_query,
    w_key,
    w_value,
    b_value,
    w_out,
    b_out,
    ln2_gain,
    ln2_bias,
    w_up,
    b_up,
    w_down,
    b_down,
    cotangent,
):
    shard = tokens[0].astype(f32)
    rows_own, width = shard.shape
    seqs = lax.axis_size("seq")
    dps = lax.axis_size("dp")
    span = 2 * rows_own
    heads, head = b_query.shape
    at_dp, at_seq, at_core = (lax.axis_index(name) for name in ("dp", "seq", "tensor"))
    flip = at_core * rows_own
    span_start = at_seq * span
    hidden_local = w_up.shape[1]
    hidden_part = hidden_local // seqs
    dp_part = width // dps
    out_part = dp_part // seqs

    ends = jnp.cumsum(lengths[0], dtype=jnp.int32)
    row_pos = span_start + (jnp.arange(span, dtype=jnp.int32) ^ flip)
    row_start = jnp.max(
        jnp.where(row_pos[:, None] >= ends[None, :], ends[None, :], 0), axis=1
    ).astype(jnp.int32)
    pos = jnp.zeros((8, span), jnp.int32).at[0].set(row_pos).at[1].set(row_start)
    first, last = jnp.min(row_start), jnp.max(row_start)
    whole_to = jnp.clip(at_seq + 1 - (last + span - 1) // span, 1, at_seq + 1)
    some_to = jnp.clip(at_seq + 1 - first // span, whole_to, at_seq + 1)
    info = jnp.stack([whole_to, some_to, at_seq, flip]).astype(jnp.int32)

    unit_one, inverse_one = norm_parts(shard)
    normed = (unit_one * ln1_gain + ln1_bias).astype(low)
    w_both = jnp.concatenate([w_key, w_value], axis=1)
    b_both = jnp.concatenate([jnp.zeros_like(b_value), b_value])
    both_own = (dot(normed, w_both) + b_both).astype(low)
    pieces = [shift_up(both_own, by) for by in range(1, seqs)]
    grad_own = cotangent[0]
    grad_own, both_own = after(grad_own, both_own)
    grad_held = [grad_own]
    for step in range(1, seqs):
        grad_held.append(shift(grad_held[-1], 1))
    grad_far = [swap(grad_own)]
    grad_act = contract_cols(jnp.concatenate([grad_own, grad_far[0]], axis=0), w_down).astype(low)
    grad_act, *pieces = after(grad_act, *pieces)
    near = jnp.stack([both_own] + pieces)
    far = swap(near)
    normed_far = swap(normed)
    normed_all = jnp.concatenate([normed, normed_far], axis=0)
    query = (dot(normed_all, w_query) + b_query.reshape(-1)).astype(low)

    if seqs > 1:
        query, grad_held[1] = after(query, grad_held[1])
    attended, lse = attend(info, query, near, far, pos, heads, head)
    if seqs > 2:
        attended, grad_held[2] = after(attended, grad_held[2])
    middle = shard + (pair_sum(dot(attended, w_out).astype(low)) + b_out)
    unit_two, inverse_two = norm_parts(middle)
    normed_two = (unit_two * ln2_gain + ln2_bias).astype(low)

    held = [normed_two]
    for step in range(1, seqs):
        held.append(shift(held[-1], 1))
    held_far = [swap(normed_two)]
    activated, grad_hidden, grad_b_up = up(held[0], held_far[0], w_up, b_up, grad_act)
    if seqs > 3:
        grad_hidden, grad_held[3] = after(grad_hidden, grad_held[3])
    grad_normed_two = contract_cols(grad_hidden, w_up).astype(low)
    grad_normed_two = pair_sum(grad_normed_two)
    result = dot(activated, w_down).astype(low)
    grad_normed_two, result, *held[1:2] = after(grad_normed_two, result, *held[1:2])

    back, grad_ln2_gain, grad_ln2_bias = norm_back(
        grad_normed_two, unit_two, inverse_two, ln2_gain
    )
    grad_out = grad_own.astype(f32)
    grad_b_down = jnp.sum(grad_out, axis=0)
    grad_middle = grad_out + back
    grad_branch = grad_middle.astype(low)
    grad_b_out = jnp.sum(grad_branch.astype(f32), axis=0)
    grad_branch_far = swap(grad_branch)
    grad_branch_all = jnp.concatenate([grad_branch, grad_branch_far], axis=0)
    grad_attended = contract_cols(grad_branch_all, w_out).astype(low)
    blocks = [at_dp ^ r for r, _ in turns]
    halves = [jnp.int32(half) for _, half in turns]
    table = jnp.stack(blocks + halves + [at_seq, at_core]).astype(jnp.int32)

    parts_out = branch_weights(
        table, grad_branch, grad_branch_far, attended, dp_part, "weight_out"
    )

    share_at = at_seq.reshape(1).astype(jnp.int32)
    acts, grads = [activated], [grad_hidden]

    def shared_part(step):
        held_far.append(swap(held[step]))
        grad_far.append(swap(grad_held[step]))
        act, grad = share(
            share_at,
            held[step],
            held_far[step],
            grad_held[step],
            grad_far[step],
            w_up,
            w_down,
            b_up,
            hidden_part,
        )
        acts.append(act)
        grads.append(grad)

    if seqs > 2:
        shared_part(1)
        grad_attended, acts[1], held[2], *parts_out = after(
            grad_attended, acts[1], held[2], *parts_out
        )
        for step in range(3, seqs):
            held[step] = shift(held[step - 1], 1)
    first_out = dp_first(parts_out, 1)

    def to_seq(item, by, axis):
        at = lax.rem(at_seq + by, seqs)
        return lax.dynamic_slice_in_dim(item, at * out_part, out_part, axis)

    grad_query, grad_both = attend_back(
        info, query, grad_attended, attended, lse, near, far, pos, heads, head
    )
    seconds = first_out[:2]
    if seqs > 1:
        grad_query, grad_both, held[-1], *seconds = after(
            grad_query, grad_both, held[-1], *seconds
        )
    last_out = dp_second(*seconds)

    for step in range(len(acts), seqs):
        shared_part(step)
    acts[-1], *last_out = after(acts[-1], *last_out)
    sum_out = dp_join(*first_out[2:], *last_out)[0]
    hidden_at = jnp.stack([at_dp ^ 3, at_dp ^ 1, at_dp ^ 2, at_dp, at_seq]).astype(jnp.int32)
    downs = hidden_weights(
        hidden_at,
        acts,
        [item for couple in zip(grad_held, grad_far) for item in couple],
        hidden_part,
        dp_part,
        "weight_down",
    )
    grads[0], sum_out, *downs = after(grads[0], sum_out, *downs)
    first_down = dp_first(downs, 1)
    narrow = sum_out.astype(low)
    out_parts = [shift(to_seq(narrow, by, 0), by) for by in range(1, seqs)]
    ups = hidden_weights(
        hidden_at,
        grads,
        [item for couple in zip(held, held_far) for item in couple],
        hidden_part,
        dp_part,
        "weight_up",
    )
    grad_query, grad_both, *rest = after(grad_query, grad_both, *first_down[:2], *ups, *out_parts)
    last_down = dp_second(*rest[:2])
    first_up = dp_first(rest[2:6], 1)
    out_parts = rest[6:]

    grad_both = grad_both.reshape(2, seqs, 2, rows_own, head)
    kept = lax.dynamic_index_in_dim(grad_both, at_core, 0, False)
    given = lax.dynamic_index_in_dim(grad_both, 1 - at_core, 0, False)
    grad_kv = (kept.astype(f32) + swap(given)[:, ::-1].astype(f32)).astype(low)
    grad_kv = grad_kv.reshape(seqs, span, head)
    total = grad_kv[0].astype(f32)
    for by in range(1, seqs):
        total = total + shift_down(grad_kv[by], by).astype(f32)
    grad_kv = total.astype(low)
    grad_qkv = jnp.concatenate([grad_query, grad_kv], axis=1)
    w_qkv = jnp.concatenate([w_query, jnp.where(at_core == 0, w_key, w_value)], axis=1)
    grad_normed = contract_cols(grad_qkv, w_qkv).astype(low)
    grad_normed, *last_down = after(grad_normed, *last_down)
    grad_normed = pair_sum(grad_normed)
    sum_down = dp_join(*first_down[2:], *last_down).astype(low)

    downs = [to_seq(sum_down, by, 2) for by in range(seqs)]
    grad_qkv, *downs = after(grad_qkv, *downs)
    downs = [downs[0]] + [shift(downs[by], by) for by in range(1, seqs)]
    parts = branch_weights(table, normed, normed_far, grad_qkv, dp_part, "weight_query")
    rest = after(*parts, *first_up[:2])
    first_query = dp_first(rest[:4], 1)
    last_up = dp_second(*rest[4:6])

    back, grad_ln1_gain, grad_ln1_bias = norm_back(
        grad_normed, unit_one, inverse_one, ln1_gain
    )
    grad_input = (grad_middle + back).astype(low)[None]
    grad_b_value = jnp.where(at_core == 1, jnp.sum(grad_kv.astype(f32), axis=0), 0.0)
    grad_b_query = jnp.sum(grad_query.astype(f32), axis=0)
    features = [
        grad_ln1_gain,
        grad_ln1_bias,
        grad_b_out,
        grad_ln2_gain,
        grad_ln2_bias,
        grad_b_down,
    ]
    count = len(features)
    features = jnp.concatenate([item.reshape(-1, head) for item in features], axis=0)
    rows = features.shape[0]
    features = features + swap(features)
    values = grad_b_value.reshape(1, head)
    values = values + swap(values)
    packed = jnp.concatenate(
        [
            features,
            grad_b_up.reshape(-1, head),
            grad_b_query.reshape(-1, head),
            jnp.broadcast_to(values, (8, head)),
        ],
        axis=0,
    )
    rest = after(packed, *last_up, *first_query[:2], *downs)
    packed, last_up, downs = rest[0], rest[1:3], rest[5:]
    last_query = dp_second(*rest[3:5])
    sum_up = dp_join(*first_up[2:], *last_up).astype(low)
    ups = [to_seq(sum_up, 0, 2)]
    for by in range(1, seqs):
        ups.append(shift(to_seq(sum_up, by, 2), by))
    total = packed + cross(packed, 1) + cross(packed, 2) + cross(packed, 3)
    total, *last_query = after(total, *last_query)
    packed = total
    for by in range(1, seqs):
        total = total + shift(packed, by)
    sum_query = dp_join(*first_query[2:], *last_query)[0]
    narrow = sum_query.astype(low)
    query_parts = [to_seq(narrow, by, 0) for by in range(1, seqs)]
    share_at, *query_parts = after(share_at, *query_parts)
    query_parts = [shift(item, by + 1) for by, item in enumerate(query_parts)]
    output = (middle + (pair_sum(result) + b_down)).astype(low)[None]
    out_w_down, out_w_up = place(share_at, downs, ups)

    out_qkv = to_seq(sum_query, 0, 0)
    for item in query_parts:
        out_qkv = out_qkv + item.astype(f32)
    out_w_out = to_seq(sum_out, 0, 0)
    for item in out_parts:
        out_w_out = out_w_out + item.astype(f32)
    out_w_out = out_w_out.T
    out_w_query = out_qkv[:, : heads * head]
    half = out_part // 2
    last_kv = out_qkv[:, heads * head :]
    mine = lax.dynamic_slice_in_dim(last_kv, at_core * half, half, 0)
    other = swap(lax.dynamic_slice_in_dim(last_kv, (1 - at_core) * half, half, 0))
    out_w_key = jnp.where(at_core == 0, mine, other)
    out_w_value = jnp.where(at_core == 0, other, mine)

    place_own = at_dp * seqs + at_seq

    def own_part(item, size, index):
        return lax.dynamic_slice_in_dim(item, index * size, size, item.ndim - 1)

    vectors = own_part(
        total[:rows].reshape(count, width), out_part // 2, place_own * 2 + at_core
    )
    thin = head // (dps * seqs)
    up_rows = b_up.shape[0]
    sum_b_up = own_part(total[rows : rows + up_rows], thin, place_own)
    sum_b_query = own_part(total[rows + up_rows : rows + up_rows + heads], thin, place_own)
    sum_b_value = own_part(total[rows + up_rows + heads], thin // 2, place_own * 2 + at_core)
    return (
        output,
        grad_input,
        vectors[0],
        vectors[1],
        out_w_query,
        sum_b_query,
        out_w_key,
        out_w_value,
        sum_b_value,
        out_w_out,
        vectors[2],
        vectors[3],
        vectors[4],
        out_w_up,
        sum_b_up,
        out_w_down,
        vectors[5],
    )


def solution(mesh):
    in_specs = (
        P("dp", ("seq", "tensor"), None),
        P("dp", None),
        P(),
        P(),
        P(None, "tensor"),
        P("tensor", None),
        P(),
        P(),
        P(),
        P("tensor", None),
        P(),
        P(),
        P(),
        P(None, "tensor"),
        P("tensor", None),
        P("tensor", None),
        P(),
        P("dp", ("seq", "tensor"), None),
    )
    out_specs = (
        P("dp", ("seq", "tensor"), None),
        P("dp", ("seq", "tensor"), None),
        P(("dp", "seq", "tensor")),
        P(("dp", "seq", "tensor")),
        P(("dp", "seq"), "tensor"),
        P("tensor", ("dp", "seq")),
        P(("dp", "seq", "tensor"), None),
        P(("dp", "seq", "tensor"), None),
        P(("dp", "seq", "tensor")),
        P("tensor", ("dp", "seq")),
        P(("dp", "seq", "tensor")),
        P(("dp", "seq", "tensor")),
        P(("dp", "seq", "tensor")),
        P(("dp", "seq"), "tensor"),
        P("tensor", ("dp", "seq")),
        P("tensor", ("dp", "seq")),
        P(("dp", "seq", "tensor")),
    )
    return jax.shard_map(
        on_device, mesh=mesh, in_specs=in_specs, out_specs=out_specs, check_vma=False
    )
```
